256 devices in a mesh: ctx: 128 (over y, x_lo, z, core), tp: 2 (over x_hi).
Axes of the slice: x: 4 (x_hi: 2, x_lo: 2; x = x_hi * 2 + x_lo), y: 4, z: 8, core: 2. Of those that a mesh axis runs over, the one named last changes fastest.
Arguments:
- query: bfloat16 [4, 64, 128], P(None, 'tp')
- keys: bfloat16 [4, 16384, 8, 128], P(None, 'ctx', 'tp'), may hold values from -6 to 6
- values: bfloat16 [4, 16384, 8, 128], P(None, 'ctx', 'tp'), may hold values from -14 to 14
- lengths: int32 [4], replicated, may hold values from 1 to 16384, as said below
- residual: bfloat16 [4, 8192], P(None, 'ctx'), may hold values from -6 to 6
- out_weight: bfloat16 [8192, 8192], P('ctx', 'tp'), may hold values from -0.0625 to 0.0625
- norm_gain: float32 [8192], replicated, may hold values from 0.1 to 1.9
- input_weight: bfloat16 [16384, 8192], P(('ctx', 'tp')), may hold values from -0.0625 to 0.0625
- gate_weight: bfloat16 [16384, 8192], P(('ctx', 'tp')), may hold values from -0.0625 to 0.0625
- conv_weight: float32 [4, 16384], P(None, ('ctx', 'tp')), may hold values from -0.8 to 0.8
- conv_bias: float32 [16384], P(('ctx', 'tp')), may hold values from -0.5 to 0.5
- conv_state: bfloat16 [4, 3, 16384], P(None, None, ('ctx', 'tp')), may hold values from -6 to 6
- proj_weight: bfloat16 [16384, 544], P(('ctx', 'tp')), may hold values from -0.046875 to 0.046875
- step_weight: bfloat16 [16384, 512], P(('ctx', 'tp')), may hold values from -0.25 to 0.25
- step_bias: float32 [16384], P(('ctx', 'tp')), may hold values from -5 to 0.5
- decay_log: float32 [16, 16384], P(None, ('ctx', 'tp')), may hold values from -1 to 2.8
- skip_gain: float32 [16384], P(('ctx', 'tp')), may hold values from 0.5 to 1.5
- scan_state: float32 [4, 16, 16384], P(None, None, ('ctx', 'tp')), may hold values from -6 to 6
- output_weight: bfloat16 [16384, 8192], P(('ctx', 'tp')), may hold values from -0.1875 to 0.1875
Outputs:
- layer_out: bfloat16 [4, 8192], P(None, ('ctx', 'tp'))
- new_state: float32 [4, 16, 16384], P(None, None, ('ctx', 'tp'))
The draws below stay inside these ranges and needn't reach their ends.
Inputs may be any that keep to these rules, and one draw needn't show every extreme that they name: `lengths`: some row has all 16384 positions live.
All inputs are finite; a program needn't handle non-finite values.
Results may differ from the reference program's by a relative error of at most 0.012.
Values may be sent and summed in bfloat16 or wider, within the bound.
A program may use at most 64 MiB of HBM per device.

```python
import jax
import jax.numpy as jnp
from jax import lax

D = 8192
QUERY_HEADS = 64
KEY_VALUE_HEADS = 8
HEAD_WIDTH = 128
DI = 16384
S = 16
R = 512
CONV = 4
DECODE_ROWS = 4
CONTEXT_LENGTH = 16384


def draw_query(key, part):
    key = jax.random.fold_in(key, 11)
    base = jax.random.normal(key, (DECODE_ROWS, QUERY_HEADS, HEAD_WIDTH), jnp.float32)
    return base.astype(jnp.bfloat16)


def rising_values(key, rise, mag_key_lo):
    sign_key, noise_key, mag_key = jax.random.split(key, 3)
    signs = jnp.where(jax.random.bernoulli(sign_key, 0.5, (KEY_VALUE_HEADS, HEAD_WIDTH)), 1.0, -1.0)
    magnitude = jax.random.uniform(mag_key, (KEY_VALUE_HEADS, HEAD_WIDTH), jnp.float32, mag_key_lo, 1.0)
    where_pos = jnp.arange(CONTEXT_LENGTH, dtype=jnp.float32) / CONTEXT_LENGTH
    profile = 0.7 * (1.0 + (rise - 1.0) * where_pos)
    noise = jnp.clip(jax.random.normal(noise_key, (DECODE_ROWS, CONTEXT_LENGTH, KEY_VALUE_HEADS, HEAD_WIDTH), jnp.float32), -6.0, 6.0)
    return profile[None, :, None, None] * (signs * magnitude)[None, None] + noise


def draw_values(key, part):
    key = jax.random.fold_in(key, 13)
    return rising_values(key, 6.0, 1.0).astype(jnp.bfloat16)


def draw_lengths(key, part):
    key = jax.random.fold_in(key, 7)
    first, second = jax.random.split(key)
    drawn = jax.random.randint(first, (DECODE_ROWS,), 1, CONTEXT_LENGTH + 1)
    chosen = jax.random.randint(second, (), 0, DECODE_ROWS)
    return jnp.where(jnp.arange(DECODE_ROWS) == chosen, CONTEXT_LENGTH, drawn).astype(jnp.int32)


def with_spikes(entries, key, source, target, parts, factor):
    def block_of(axis_at):
        return (jnp.arange(entries.shape[axis_at]) // (entries.shape[axis_at] // parts)).reshape((-1,) + (1,) * (entries.ndim - 1 - axis_at))

    one_side = jax.random.permutation(key, parts)[block_of(target)]
    second = (block_of(target) + parts // 2) % parts
    return jnp.where((block_of(source) == one_side) | (block_of(source) == second), factor * entries, entries)


def block_levels(stream_key, shape, cuts, smallest, high):
    gain, own = 1.0, jax.random.fold_in(stream_key, 6)
    for position, parts in cuts:
        draws = jnp.exp(jax.random.uniform(jax.random.fold_in(own, position), (parts,), jnp.float32, smallest / len(cuts), high / len(cuts)))
        gain = gain * jnp.repeat(draws, shape[position] // parts).reshape([-1 if axis == position else 1 for axis in range(len(shape))])
    return gain


def gaussian(key, extent, width, reach, cuts=(), kind=jnp.bfloat16):
    result = jax.random.normal(key, extent, jnp.float32) * width
    if len(cuts) > 0:
        result = block_levels(key, extent, cuts, -0.22, 0.18) * result
    return jnp.clip(result, min=-reach, max=reach).astype(kind)


def gaussian_with(own_key, shape, scale, limit, pieces, heavy, kind=jnp.bfloat16):
    values = scale * jax.random.normal(own_key, shape, jnp.float32)
    if pieces:
        values = values * block_levels(own_key, shape, pieces, -0.22, 0.18)
    return jnp.clip(with_spikes(values, jax.random.fold_in(own_key, 3), *heavy), -limit, limit).astype(kind)


def setup_inputs(seed: int = 0) -> dict:
    seeds = jax.random.split(jax.random.key(seed), 20)
    return {
        "query": draw_query(jax.random.fold_in(seeds[19], 71), 0),
        "keys": gaussian(seeds[1], (DECODE_ROWS, CONTEXT_LENGTH, KEY_VALUE_HEADS, HEAD_WIDTH), 1.0, 6.0, ((1, 128), (2, 2))),
        "values": draw_values(jax.random.fold_in(seeds[19], 71), 0),
        "lengths": draw_lengths(jax.random.fold_in(seeds[19], 71), 0),
        "residual": gaussian(seeds[4], (DECODE_ROWS, D), 1.0, 6.0, ((1, 128),)),
        "out_weight": gaussian(seeds[5], (D, QUERY_HEADS * HEAD_WIDTH), (QUERY_HEADS * HEAD_WIDTH) ** -0.5, 0.0625, ((0, 128), (1, 2))),
        "norm_gain": jnp.clip(1.0 + 0.18 * jax.random.normal(seeds[6], (D,), jnp.float32), 0.1, 1.9),
        "input_weight": gaussian(seeds[7], (DI, D), D ** -0.5, 0.0625, ((0, 256),)),
        "gate_weight": gaussian(seeds[8], (DI, D), D ** -0.5, 0.0625, ((0, 256),)),
        "conv_weight": jnp.clip(jax.random.uniform(seeds[9], (CONV, DI), jnp.float32, -0.8, 0.8) * block_levels(seeds[9], (CONV, DI), ((1, 256),), -0.4, 0.0), -0.8, 0.8),
        "conv_bias": jnp.clip(jax.random.uniform(seeds[10], (DI,), jnp.float32, -0.5, 0.5) * block_levels(seeds[10], (DI,), ((0, 256),), -0.4, 0.0), -0.5, 0.5),
        "conv_state": gaussian(seeds[11], (DECODE_ROWS, CONV - 1, DI), 1.0, 6.0, ((2, 256),)),
        "proj_weight": gaussian(seeds[12], (DI, R + 2 * S), DI ** -0.5, 0.046875, ((0, 256),)),
        "step_weight": gaussian(seeds[13], (DI, R), R ** -0.5, 0.25, ((0, 256),)),
        "step_bias": jnp.clip(-5.0 + 5.5 * jax.random.uniform(seeds[14], (DI,), jnp.float32) ** block_levels(seeds[14], (DI,), ((0, 256),), -0.2, 0.2), -5.0, 0.5),
        "decay_log": jnp.clip(-1.0 + 3.8 * jax.random.uniform(seeds[15], (S, DI), jnp.float32) ** block_levels(seeds[15], (S, DI), ((1, 256),), -0.2, 0.2), -1.0, 2.8),
        "skip_gain": jnp.clip(0.5 + 1.0 * jax.random.uniform(seeds[16], (DI,), jnp.float32) ** block_levels(seeds[16], (DI,), ((0, 256),), -0.2, 0.2), 0.5, 1.5),
        "scan_state": gaussian(seeds[17], (DECODE_ROWS, S, DI), 1.0, 6.0, ((2, 256),), jnp.float32),
        "output_weight": gaussian_with(seeds[18], (DI, D), DI ** -0.5, 0.1875, ((0, 256),), (0, 1, 256, 6.0)),
    }


def times_rows(left, right):
    return lax.dot_general(left, right, (((1,), (1,)), ((), ())), preferred_element_type=jnp.float32)

def reference(query, keys, values, lengths, residual, out_weight, norm_gain, input_weight, gate_weight, conv_weight, conv_bias, conv_state, proj_weight, step_weight, step_bias, decay_log, skip_gain, scan_state, output_weight):
    decode_row_count = query.shape[0]
    query_group_width = QUERY_HEADS // KEY_VALUE_HEADS
    query_rows = query.astype(jnp.float32).reshape(decode_row_count, KEY_VALUE_HEADS, query_group_width, HEAD_WIDTH)
    scores = jnp.einsum('rkgd,rtkd->rkgt', query_rows, keys.astype(jnp.float32)) * HEAD_WIDTH ** (-0.5)
    positions = jnp.arange(CONTEXT_LENGTH, dtype=jnp.int32)
    live = (positions[None, :] < lengths[:, None])[:, None, None, :]
    scores = jnp.where(live, scores, -1e+30)
    highest = lax.optimization_barrier(jnp.max(scores, axis=-1, keepdims=True))
    weights = jnp.exp(scores - highest) * live.astype(jnp.float32)
    totals = lax.optimization_barrier(jnp.sum(weights, axis=-1))
    summed = jnp.einsum('rkgt,rtkd->rkgd', weights, values.astype(jnp.float32))
    attended = (summed / totals[..., None]).astype(jnp.bfloat16).reshape(decode_row_count, QUERY_HEADS * HEAD_WIDTH)
    hidden = (residual.astype(jnp.float32) + times_rows(attended, out_weight)).astype(jnp.bfloat16)
    wide = hidden.astype(jnp.float32)
    meansq = lax.optimization_barrier(jnp.mean(wide * wide, axis=-1, keepdims=True))
    normed = (wide * lax.rsqrt(meansq + 1e-05) * norm_gain).astype(jnp.bfloat16)
    inputs = times_rows(normed, input_weight)
    gates = times_rows(normed, gate_weight)
    window = jnp.concatenate([conv_state.astype(jnp.float32), inputs[:, None, :]], axis=1)
    mixed_in = jax.nn.silu(lax.optimization_barrier(jnp.sum(window * conv_weight[None], axis=1)) + conv_bias)
    projected = jnp.dot(mixed_in.astype(jnp.bfloat16), proj_weight, preferred_element_type=jnp.float32)
    rank_part = projected[:, :R].astype(jnp.bfloat16)
    entry_map = projected[:, R:R + S]
    exit_map = projected[:, R + S:]
    step = jax.nn.softplus(times_rows(rank_part, step_weight) + step_bias)
    decay = jnp.exp(-step[:, None, :] * jnp.exp(decay_log)[None])
    new_state = decay * scan_state + step[:, None, :] * entry_map[:, :, None] * mixed_in[:, None, :]
    gated = ((lax.optimization_barrier(jnp.sum(new_state * exit_map[:, :, None], axis=1)) + skip_gain * mixed_in) * jax.nn.silu(gates)).astype(jnp.bfloat16)
    layer_out = (hidden.astype(jnp.float32) + jnp.dot(gated, output_weight, preferred_element_type=jnp.float32)).astype(jnp.bfloat16)
    return (layer_out, new_state)
```

```python
import functools

import jax
import jax.numpy as jnp
from jax import lax
from jax.experimental import pallas as pl
from jax.experimental.pallas import tpu as pltpu
from jax.sharding import PartitionSpec as P

MESH = pl.DeviceIdType.MESH
F32 = jnp.float32
BF16 = jnp.bfloat16


def far_first(n):
    return sorted(range(1, n), key=lambda d: -min(d, n - d))


def nt(left, right):
    return lax.dot_general(
        left, right, (((1,), (1,)), ((), ())), preferred_element_type=F32
    )


def silu(x):
    return x * (1.0 / (1.0 + jnp.exp(-x)))


def softplus(x):
    return jnp.maximum(x, 0.0) + jnp.log1p(jnp.exp(-jnp.abs(x)))


def iota(shape, dim):
    return lax.broadcasted_iota(jnp.int32, shape, dim)


def kernel(*refs):
    names_in = (
        "q", "k", "v", "res", "ow", "gain", "iw", "gw", "cw", "cb", "cs", "pw",
        "sw", "sb", "dl", "sg", "ss", "outw",
    )
    n_in = len(names_in)
    lengths = refs[0]
    hbm = dict(zip(names_in, refs[1 : 1 + n_in]))
    lo_ref, ns_ref = refs[1 + n_in : 3 + n_in]
    vm = dict(zip(names_in, refs[3 + n_in : 3 + 2 * n_in]))
    (
        obuf, r_o, ob, mlb, att, attf, hb, w2, p_a, r_pa, p_b, r_pb,
        tb, r_t, tz, r_z, tc, r_c, nsb, in_sem, send_sem, recv_sem, out_sem,
    ) = refs[3 + 2 * n_in :]

    c = lax.axis_index("ctx")
    h = lax.axis_index("tp")
    a = lax.div(c, 16)
    b = lax.rem(c, 16)
    z = lax.div(b, 2)
    core = lax.rem(b, 2)
    e = a * 2 + h

    def in_a8(d):
        other = lax.rem(a + d, 8)
        return other, (other * 16 + b, h)

    def in_a16(d):
        other = lax.rem(e + d, 16)
        return other, (lax.div(other, 2) * 16 + b, lax.rem(other, 2))

    def in_b16(d):
        other = lax.rem(b + d, 16)
        return other, (a * 16 + other, h)

    def in_z(d):
        other = lax.rem(z + d, 8)
        return other, (a * 16 + other * 2 + core, h)

    corners = (
        (a * 16 + b, 1 - h),
        (a * 16 + z * 2 + (1 - core), h),
        (a * 16 + z * 2 + (1 - core), 1 - h),
    )

    loads = {
        name: pltpu.make_async_copy(hbm[name], vm[name], in_sem.at[i])
        for i, name in enumerate(names_in)
    }
    for name in names_in:
        loads[name].start()

    barrier = pltpu.get_barrier_semaphore()
    greeted = [in_a16(d)[1] for d in far_first(16)]
    greeted += [in_b16(d)[1] for d in far_first(16)] + [corners[2]]
    for peer in greeted:
        pl.semaphore_signal(barrier, 1, device_id=peer, device_id_type=MESH)

    def send(src, dst, stage, peer):
        pltpu.make_async_remote_copy(
            src, dst, send_sem.at[stage], recv_sem.at[stage],
            device_id=peer, device_id_type=MESH,
        ).start()

    def arrived(block, stage):
        pltpu.make_async_copy(block, block, recv_sem.at[stage]).wait()

    def sent(block, stage):
        pltpu.make_async_copy(block, block, send_sem.at[stage]).wait()

    for name in ("q", "k", "v"):
        loads[name].wait()
    shape = (32, 512)
    column = iota(shape, 1)
    same_head = lax.rem(column, 4) == lax.div(iota(shape, 0), 8)
    position = c * 128 + lax.div(column, 4)
    lane16 = iota((16, 128), 1)
    for r in range(4):
        scores = nt(vm["q"][r], vm["k"][r]) * (128.0 ** -0.5)
        live = jnp.logical_and(same_head, position < lengths[r])
        scores = jnp.where(live, scores, -1e30)
        high = jnp.max(scores, axis=1, keepdims=True)
        weights = jnp.where(live, jnp.exp(scores - high), 0.0)
        total = jnp.sum(weights, axis=1, keepdims=True)
        summed = jnp.dot(
            weights.astype(BF16), vm["v"][r], preferred_element_type=F32
        )
        for half in range(2):
            rows = slice(half * 16, half * 16 + 16)
            obuf[2 * r + half, 0] = summed[rows]
            obuf[2 * r + half, 1] = jnp.where(lane16 < 64, high[rows], total[rows])

    pl.semaphore_wait(barrier, len(greeted))

    for d in far_first(8):
        other, peer = in_a8(d)
        send(obuf.at[other], r_o.at[d - 1], 0, peer)
    arrived(r_o, 0)
    parts = [(obuf[a, 0], obuf[a, 1])] + [(r_o[i, 0], r_o[i, 1]) for i in range(7)]
    highs = [ml[:, 0:1] for _, ml in parts]
    totals = [ml[:, 64:65] for _, ml in parts]
    top = functools.reduce(jnp.maximum, highs)
    scales = [jnp.exp(high - top) for high in highs]
    total = sum(s * t for s, t in zip(scales, totals))
    summed = sum(s * o for s, (o, _) in zip(scales, parts))

    on_diag = lane16 == iota((16, 128), 0)
    ob[b] = summed.astype(BF16)
    mlb[b, 0:1] = jnp.sum(jnp.where(on_diag, top, 0.0), axis=0, keepdims=True)
    mlb[b, 1:2] = jnp.sum(jnp.where(on_diag, total, 0.0), axis=0, keepdims=True)
    for d in far_first(16):
        _, peer = in_b16(d)
        send(mlb.at[b], mlb.at[b], 1, peer)
        send(ob.at[b], ob.at[b], 2, peer)
    arrived(mlb.at[pl.ds(0, 15)], 1)
    high_rows = mlb[:, 0, :]
    total_rows = mlb[:, 1, :]
    scale_rows = jnp.exp(high_rows - jnp.max(high_rows, axis=0, keepdims=True))
    all_total = jnp.sum(scale_rows * total_rows, axis=0, keepdims=True)
    valid = iota((1, 128), 1) < 16
    scale_rows = scale_rows / jnp.where(valid, all_total, 1.0)
    columns = [
        jnp.sum(jnp.where(on_diag, scale_rows[i : i + 1], 0.0), axis=1, keepdims=True)
        for i in range(16)
    ]
    arrived(ob.at[pl.ds(0, 15)], 2)
    attended = sum(columns[i] * ob[i].astype(F32) for i in range(16))

    att[a] = attended.astype(BF16)
    for d in far_first(8):
        _, peer = in_a8(d)
        send(att.at[a], att.at[a], 3, peer)
    loads["ow"].wait()
    loads["res"].wait()
    arrived(att.at[pl.ds(0, 7)], 3)
    for i in range(8):
        attf[i // 2, (i % 2) * 16 : (i % 2) * 16 + 16] = att[i].astype(F32)
    flat = jnp.concatenate([attf[:, i, :] for i in range(32)], axis=1).astype(BF16)
    partial = nt(flat, vm["ow"][...])
    partial = partial + jnp.where(h == 0, vm["res"][...].astype(F32), 0.0)

    twice = jnp.concatenate([partial, partial], axis=1)
    hb[b] = jnp.where(lax.div(iota((4, 128), 1), 64) == core, twice, 0.0)
    for d in far_first(16):
        _, peer = in_b16(d)
        send(hb.at[b], hb.at[b], 4, peer)
    arrived(hb.at[pl.ds(0, 15)], 4)
    halves = hb[...].reshape(8, 2, 4, 128)
    w2[e] = halves[:, 0] + halves[:, 1]
    for d in far_first(16):
        _, peer = in_a16(d)
        send(w2.at[e], w2.at[e], 5, peer)
    for name in ("gain", "iw", "gw", "cw", "cb", "cs", "pw"):
        loads[name].wait()
    conv = vm["cb"][...]
    for i in range(3):
        conv = conv + vm["cs"][i].astype(F32) * vm["cw"][i : i + 1]
    arrived(w2.at[pl.ds(0, 15)], 5)
    pairs = w2[...].reshape(8, 2, 8, 4, 128)
    hidden = (pairs[:, 0] + pairs[:, 1]).astype(BF16).astype(F32)
    square = jnp.sum(jnp.sum(hidden * hidden, axis=(0, 1)), axis=1, keepdims=True)
    scale = lax.rsqrt(square * (1.0 / 8192.0) + 1e-5)
    gain = vm["gain"][...]
    normed = jnp.concatenate(
        [
            hidden[i // 8, i % 8] * scale * gain[i : i + 1]
            for i in range(64)
        ],
        axis=1,
    ).astype(BF16)
    inputs = nt(normed, vm["iw"][...])
    mixed = silu(conv + inputs * vm["cw"][3:4])

    local = jnp.dot(mixed.astype(BF16), vm["pw"][...], preferred_element_type=F32)
    for i in range(4):
        p_a[i] = local[:, i * 128 : i * 128 + 128]
    p_a[4] = jnp.concatenate([local[:, 512:544], jnp.zeros((4, 96), F32)], axis=1)
    for d in far_first(16):
        _, peer = in_a16(d)
        send(p_a, r_pa.at[d - 1], 6, peer)
    gates = silu(nt(normed, vm["gw"][...]))
    for name in ("sw", "sb", "dl", "sg", "ss", "outw"):
        loads[name].wait()
    rate = jnp.exp(vm["dl"][...])
    arrived(r_pa, 6)
    p_b[...] = p_a[...] + jnp.sum(r_pa[...], axis=0)
    for d in far_first(16):
        _, peer = in_b16(d)
        send(p_b, r_pb.at[d - 1], 7, peer)
    arrived(r_pb, 7)
    projected = p_b[...] + jnp.sum(r_pb[...], axis=0)

    rank = jnp.concatenate([projected[i] for i in range(4)], axis=1).astype(BF16)
    step = softplus(nt(rank, vm["sw"][...]) + vm["sb"][...])
    maps = projected[4]
    pick_exit = lane16 == iota((16, 128), 0) + 16
    skip = vm["sg"][...] * mixed
    rows = []
    for r in range(4):
        entry = jnp.sum(jnp.where(on_diag, maps[r : r + 1], 0.0), axis=1, keepdims=True)
        leave = jnp.sum(jnp.where(pick_exit, maps[r : r + 1], 0.0), axis=1, keepdims=True)
        step_r = step[r : r + 1]
        state = jnp.exp(-step_r * rate) * vm["ss"][r] + entry * (step_r * mixed[r : r + 1])
        nsb[r] = state
        rows.append(jnp.sum(state * leave, axis=0, keepdims=True))
    store = pltpu.make_async_copy(nsb, ns_ref, out_sem)
    store.start()
    gated = ((jnp.concatenate(rows, axis=0) + skip) * gates).astype(BF16)

    term = jnp.dot(gated, vm["outw"][...], preferred_element_type=F32)
    for i in range(64):
        tb[i // 8, i % 8] = term[:, i * 128 : i * 128 + 128]
    for d in far_first(8):
        other, peer = in_a8(d)
        send(tb.at[other], r_t.at[d - 1], 8, peer)
    arrived(r_t, 8)
    tz[...] = tb[a] + jnp.sum(r_t[...], axis=0)
    for d in far_first(8):
        other, peer = in_z(d)
        send(tz.at[other], r_z.at[d - 1], 9, peer)
    arrived(r_z, 9)
    tc[...] = tz[z] + jnp.sum(r_z[...], axis=0)
    for i, peer in enumerate(corners):
        send(tc, r_c.at[i], 10, peer)
    own = (w2[2 * a, z] + w2[2 * a + 1, z]).astype(BF16).astype(F32)
    arrived(r_c, 10)
    whole = tc[...] + jnp.sum(r_c[...], axis=0) + own
    place = core * 2 + h
    picked = whole[:, 0:32]
    for i in range(1, 4):
        picked = jnp.where(place == i, whole[:, i * 32 : i * 32 + 32], picked)
    lo_ref[...] = picked

    store.wait()
    sent(r_o, 0)
    sent(mlb.at[pl.ds(0, 15)], 1)
    sent(ob.at[pl.ds(0, 15)], 2)
    sent(att.at[pl.ds(0, 7)], 3)
    sent(hb.at[pl.ds(0, 15)], 4)
    sent(w2.at[pl.ds(0, 15)], 5)
    sent(r_pa, 6)
    sent(r_pb, 7)
    sent(r_t, 8)
    sent(r_z, 9)
    sent(r_c, 10)


def on_device(
    query, keys, values, lengths, residual, out_weight, norm_gain, input_weight,
    gate_weight, conv_weight, conv_bias, conv_state, proj_weight, step_weight,
    step_bias, decay_log, skip_gain, scan_state, output_weight,
):
    operands = (
        query,
        keys.reshape(4, 512, 128),
        values.reshape(4, 512, 128),
        residual,
        out_weight,
        norm_gain.reshape(64, 128),
        input_weight,
        gate_weight,
        conv_weight,
        conv_bias.reshape(1, 64),
        conv_state.transpose(1, 0, 2),
        proj_weight,
        step_weight,
        step_bias.reshape(1, 64),
        decay_log,
        skip_gain.reshape(1, 64),
        scan_state,
        output_weight,
    )
    vmem = [pltpu.VMEM(x.shape, x.dtype) for x in operands]
    scratch = [
        pltpu.VMEM((8, 2, 16, 128), F32),
        pltpu.VMEM((7, 2, 16, 128), F32),
        pltpu.VMEM((16, 16, 128), BF16),
        pltpu.VMEM((16, 2, 128), F32),
        pltpu.VMEM((8, 16, 128), BF16),
        pltpu.VMEM((4, 32, 128), F32),
        pltpu.VMEM((16, 4, 128), F32),
        pltpu.VMEM((16, 8, 4, 128), F32),
        pltpu.VMEM((5, 4, 128), F32),
        pltpu.VMEM((15, 5, 4, 128), F32),
        pltpu.VMEM((5, 4, 128), F32),
        pltpu.VMEM((15, 5, 4, 128), F32),
        pltpu.VMEM((8, 8, 4, 128), F32),
        pltpu.VMEM((7, 8, 4, 128), F32),
        pltpu.VMEM((8, 4, 128), F32),
        pltpu.VMEM((7, 4, 128), F32),
        pltpu.VMEM((4, 128), F32),
        pltpu.VMEM((3, 4, 128), F32),
        pltpu.VMEM((4, 16, 64), F32),
        pltpu.SemaphoreType.DMA((len(operands),)),
        pltpu.SemaphoreType.DMA((11,)),
        pltpu.SemaphoreType.DMA((11,)),
        pltpu.SemaphoreType.DMA,
    ]
    layer_out, new_state = pl.pallas_call(
        kernel,
        out_shape=(
            jax.ShapeDtypeStruct((4, 32), F32),
            jax.ShapeDtypeStruct((4, 16, 64), F32),
        ),
        in_specs=[pl.BlockSpec(memory_space=pltpu.SMEM)]
        + [pl.BlockSpec(memory_space=pltpu.HBM)] * len(operands),
        out_specs=(
            pl.BlockSpec(memory_space=pltpu.VMEM),
            pl.BlockSpec(memory_space=pltpu.HBM),
        ),
        scratch_shapes=vmem + scratch,
        compiler_params=pltpu.CompilerParams(
            collective_id=0, has_side_effects=True, vmem_limit_bytes=56 << 20
        ),
        name="decode_step",
    )(lengths, *operands)
    return layer_out.astype(BF16), new_state


def solution(mesh):
    placed = (
        P(None, "tp", None),
        P(None, "ctx", "tp", None),
        P(None, "ctx", "tp", None),
        P(),
        P(None, "ctx"),
        P("ctx", "tp"),
        P(),
        P(("ctx", "tp"), None),
        P(("ctx", "tp"), None),
        P(None, ("ctx", "tp")),
        P(("ctx", "tp")),
        P(None, None, ("ctx", "tp")),
        P(("ctx", "tp"), None),
        P(("ctx", "tp"), None),
        P(("ctx", "tp")),
        P(None, ("ctx", "tp")),
        P(("ctx", "tp")),
        P(None, None, ("ctx", "tp")),
        P(("ctx", "tp"), None),
    )
    return jax.shard_map(
        on_device,
        mesh=mesh,
        in_specs=placed,
        out_specs=(P(None, ("ctx", "tp")), P(None, None, ("ctx", "tp"))),
        check_vma=False,
    )
```

```python
import functools

import jax
import jax.numpy as jnp
from jax import lax
from jax.experimental import pallas as pl
from jax.experimental.pallas import tpu as pltpu
from jax.sharding import PartitionSpec as P

MESH = pl.DeviceIdType.MESH
F32 = jnp.float32
BF16 = jnp.bfloat16


def far_first(n):
    return sorted(range(1, n), key=lambda d: -min(d, n - d))


def nt(left, right):
    return lax.dot_general(
        left, right, (((1,), (1,)), ((), ())), preferred_element_type=F32
    )


def silu(x):
    return x * (1.0 / (1.0 + jnp.exp(-x)))


def softplus(x):
    return jnp.maximum(x, 0.0) + jnp.log1p(jnp.exp(-jnp.abs(x)))


def iota(shape, dim):
    return lax.broadcasted_iota(jnp.int32, shape, dim)


def kernel(*refs):
    names_in = (
        "len", "q", "k", "v", "res", "ow", "gain", "iw", "gw", "cw", "cb", "cs",
        "pw", "sw", "sb", "dl", "sg", "ss", "outw",
    )
    n_in = len(names_in)
    hbm = dict(zip(names_in, refs[:n_in]))
    lo_ref, ns_ref = refs[n_in : 2 + n_in]
    vm = dict(zip(names_in, refs[2 + n_in : 2 + 2 * n_in]))
    (
        obuf, r_o, mid, r_m, att, hb, w2, p_a, r_pa, rank_b, r_rank, maps_b,
        r_maps, tb, r_t, tz, r_z, in_sem, send_sem, recv_sem,
    ) = refs[2 + 2 * n_in :]

    c = lax.axis_index("ctx")
    h = lax.axis_index("tp")
    a = lax.div(c, 16)
    b = lax.rem(c, 16)
    z = lax.div(b, 2)
    core = lax.rem(b, 2)
    e = a * 2 + h
    g = a * 2 + core

    def in_yx(d):
        other = lax.rem(e + d, 16)
        return other, (lax.div(other, 2) * 16 + b, lax.rem(other, 2))

    def in_b16(d):
        other = lax.rem(b + d, 16)
        return other, (a * 16 + other, h)

    def in_g16(d):
        other = lax.rem(g + d, 16)
        return other, (lax.div(other, 2) * 16 + z * 2 + lax.rem(other, 2), h)

    def in_z(d):
        other = lax.rem(z + d, 8)
        return other, (a * 16 + other * 2 + core, h)

    loads = {
        name: pltpu.make_async_copy(hbm[name], vm[name], in_sem.at[i])
        for i, name in enumerate(names_in)
    }

    def need(*names):
        for name in names:
            loads.pop(name).wait()

    first = ("k", "q", "len", "v")
    for name in first:
        loads[name].start()

    barrier = pltpu.get_barrier_semaphore()
    greeted = [in_b16(d)[1] for d in far_first(16)]
    greeted += [in_yx(d)[1] for d in far_first(16)]
    greeted += [
        (lax.rem(a + d, 8) * 16 + z * 2 + (1 - core), h) for d in far_first(8)
    ]
    for peer in greeted:
        pl.semaphore_signal(barrier, 1, device_id=peer, device_id_type=MESH)

    def send(src, dst, stage, peer):
        pltpu.make_async_remote_copy(
            src, dst, send_sem.at[stage], recv_sem.at[stage],
            device_id=peer, device_id_type=MESH,
        ).start()

    def arrived(block, stage):
        pltpu.make_async_copy(block, block, recv_sem.at[stage]).wait()

    pending = []

    def sent(block, stage):
        pltpu.make_async_copy(block, block, send_sem.at[stage]).wait()

    shape = (32, 512)
    column = iota(shape, 1)
    same_head = lax.rem(column, 4) == lax.div(iota(shape, 0), 8)
    position = c * 128 + lax.div(column, 4)
    lane8 = iota((8, 128), 1)
    need(*first)
    for r in range(4):
        scores = nt(vm["q"][r], vm["k"][r]) * (128.0 ** -0.5)
        live = jnp.logical_and(same_head, position < vm["len"][r])
        scores = jnp.where(live, scores, -1e30)
        high = jnp.max(scores, axis=1, keepdims=True)
        weights = jnp.where(live, jnp.exp(scores - high), 0.0)
        total = jnp.sum(weights, axis=1, keepdims=True)
        summed = jnp.dot(
            weights.astype(BF16), vm["v"][r], preferred_element_type=F32
        )
        for i in range(4):
            rows = slice(i * 8, i * 8 + 8)
            obuf[4 * r + i, 0] = summed[rows]
            obuf[4 * r + i, 1] = jnp.where(lane8 < 64, high[rows], total[rows])

    pl.semaphore_wait(barrier, len(greeted))

    for d in far_first(16):
        other, peer = in_g16(d)
        send(obuf.at[other], r_o.at[d - 1], 0, peer)
    pending.append((r_o, 0))
    for name in names_in:
        if name not in first:
            loads[name].start()

    def merge(parts):
        highs = [ml[:, 0:1] for _, ml in parts]
        totals = [ml[:, 64:65] for _, ml in parts]
        top = functools.reduce(jnp.maximum, highs)
        scales = [jnp.exp(high - top) for high in highs]
        total = sum(s * t for s, t in zip(scales, totals))
        return top, total, sum(s * o for s, (o, _) in zip(scales, parts))

    arrived(r_o, 0)
    top, total, summed = merge(
        [(obuf[g, 0], obuf[g, 1])] + [(r_o[i, 0], r_o[i, 1]) for i in range(15)]
    )
    mid[0] = summed
    mid[1] = jnp.where(lane8 < 64, top, total)

    for d in far_first(8):
        _, peer = in_z(d)
        send(mid, r_m.at[d - 1], 1, peer)
    pending.append((r_m, 1))
    arrived(r_m, 1)
    _, total, summed = merge(
        [(mid[0], mid[1])] + [(r_m[i, 0], r_m[i, 1]) for i in range(7)]
    )

    att[g] = summed / total
    for d in far_first(16):
        _, peer = in_g16(d)
        send(att.at[g], att.at[g], 2, peer)
    pending.append((att.at[pl.ds(0, 15)], 2))
    need("ow", "res")
    arrived(att.at[pl.ds(0, 15)], 2)
    heads = att[...].reshape(4, 4, 8, 128)
    flat = jnp.concatenate(
        [heads[:, i // 8, i % 8, :] for i in range(32)], axis=1
    ).astype(BF16)
    partial = nt(flat, vm["ow"][...])
    partial = partial + jnp.where(h == 0, vm["res"][...].astype(F32), 0.0)

    twice = jnp.concatenate([partial, partial], axis=1)
    hb[b] = jnp.where(lax.div(iota((4, 128), 1), 64) == core, twice, 0.0)
    for d in far_first(16):
        _, peer = in_b16(d)
        send(hb.at[b], hb.at[b], 4, peer)
    pending.append((hb.at[pl.ds(0, 15)], 4))
    arrived(hb.at[pl.ds(0, 15)], 4)
    halves = hb[...].reshape(8, 2, 4, 128)
    w2[e] = (halves[:, 0] + halves[:, 1]).reshape(32, 128).astype(BF16)
    for d in far_first(16):
        _, peer = in_yx(d)
        send(w2.at[e], w2.at[e], 5, peer)
    pending.append((w2.at[pl.ds(0, 15)], 5))
    need("gain", "iw", "gw", "cw", "cb", "cs", "pw")
    conv = vm["cb"][...]
    for i in range(3):
        conv = conv + vm["cs"][i].astype(F32) * vm["cw"][i : i + 1]
    arrived(w2.at[pl.ds(0, 15)], 5)

    def whole_hidden(block):
        both = w2[2 * block].astype(F32) + w2[2 * block + 1].astype(F32)
        return both.astype(BF16).astype(F32)

    hidden = [whole_hidden(i) for i in range(8)]
    squares = jnp.sum(sum(x * x for x in hidden), axis=1, keepdims=True)
    square = sum(squares[i * 4 : i * 4 + 4] for i in range(8))
    scale = lax.rsqrt(square * (1.0 / 8192.0) + 1e-5)
    gain = vm["gain"][...]
    normed = jnp.concatenate(
        [
            hidden[i // 8][i % 8 * 4 : i % 8 * 4 + 4] * scale * gain[i : i + 1]
            for i in range(64)
        ],
        axis=1,
    ).astype(BF16)
    inputs = nt(normed, vm["iw"][...])
    mixed = silu(conv + inputs * vm["cw"][3:4])

    local = jnp.dot(mixed.astype(BF16), vm["pw"][...], preferred_element_type=F32)
    for i in range(4):
        p_a[i] = local[:, i * 128 : i * 128 + 128]
    p_a[4] = jnp.concatenate([local[:, 512:544], jnp.zeros((4, 96), F32)], axis=1)
    for d in far_first(16):
        _, peer = in_yx(d)
        send(p_a, r_pa.at[d - 1], 6, peer)
    pending.append((r_pa, 6))
    gates = silu(nt(normed, vm["gw"][...]))
    need("sw", "sb", "dl", "sg", "ss", "outw")
    rate = jnp.exp(vm["dl"][...])
    skip = vm["sg"][...] * mixed
    arrived(r_pa, 6)
    projected = p_a[...] + jnp.sum(r_pa[...], axis=0)
    ranks = projected[0:4].reshape(16, 128)
    rank_b[...] = ranks.astype(BF16)
    maps_b[...] = projected[4]
    for d in far_first(16):
        _, peer = in_b16(d)
        send(rank_b, r_rank.at[d - 1], 7, peer)
        send(maps_b, r_maps.at[d - 1], 8, peer)
    pending.append((r_rank, 7))
    pending.append((r_maps, 8))
    arrived(r_rank, 7)
    ranks = ranks + jnp.sum(r_rank[...].astype(F32), axis=0)
    arrived(r_maps, 8)
    maps = maps_b[...] + jnp.sum(r_maps[...], axis=0)

    rank = jnp.concatenate(
        [ranks[i * 4 : i * 4 + 4] for i in range(4)], axis=1
    ).astype(BF16)
    step = softplus(nt(rank, vm["sw"][...]) + vm["sb"][...])
    lane16 = iota((16, 128), 1)
    pick_entry = lane16 == iota((16, 128), 0)
    pick_leave = lane16 == iota((16, 128), 0) + 16
    rows = []
    for r in range(4):
        row = maps[r : r + 1]
        entry = jnp.sum(jnp.where(pick_entry, row, 0.0), axis=1, keepdims=True)
        leave = jnp.sum(jnp.where(pick_leave, row, 0.0), axis=1, keepdims=True)
        step_r = step[r : r + 1]
        state = jnp.exp(-step_r * rate) * vm["ss"][r] + entry * (step_r * mixed[r : r + 1])
        ns_ref[r] = state
        rows.append(jnp.sum(state * leave, axis=0, keepdims=True))
    gated = ((jnp.concatenate(rows, axis=0) + skip) * gates).astype(BF16)

    term = jnp.dot(gated, vm["outw"][...], preferred_element_type=F32)
    for i in range(8):
        tb[i] = jnp.concatenate(
            [
                term[:, (i * 8 + k) * 128 : (i * 8 + k) * 128 + 128]
                for k in range(8)
            ],
            axis=0,
        ).astype(BF16)
    for d in far_first(16):
        other, peer = in_yx(d)
        send(tb.at[lax.div(other, 2)], r_t.at[d - 1], 9, peer)
    pending.append((r_t, 9))
    mine = whole_hidden(a)
    own = sum(
        jnp.where(z == i, mine[i * 4 : i * 4 + 4], 0.0) for i in range(8)
    )
    arrived(r_t, 9)
    summed = tb[a].astype(F32) + jnp.sum(r_t[...].astype(F32), axis=0)
    tz[...] = summed.reshape(8, 4, 128)
    for d in far_first(16):
        other, peer = in_b16(d)
        send(tz.at[lax.div(other, 2)], r_z.at[d - 1], 10, peer)
    pending.append((r_z, 10))
    arrived(r_z, 10)
    whole = tz[z] + jnp.sum(r_z[...], axis=0) + own
    place = core * 2 + h
    picked = whole[:, 0:32]
    for i in range(1, 4):
        picked = jnp.where(place == i, whole[:, i * 32 : i * 32 + 32], picked)
    lo_ref[...] = picked

    for block, stage in pending:
        sent(block, stage)


def on_device(
    query, keys, values, lengths, residual, out_weight, norm_gain, input_weight,
    gate_weight, conv_weight, conv_bias, conv_state, proj_weight, step_weight,
    step_bias, decay_log, skip_gain, scan_state, output_weight,
):
    operands = (
        lengths,
        query,
        keys.reshape(4, 512, 128),
        values.reshape(4, 512, 128),
        residual,
        out_weight,
        norm_gain.reshape(64, 128),
        input_weight,
        gate_weight,
        conv_weight,
        conv_bias.reshape(1, 64),
        conv_state.transpose(1, 0, 2),
        proj_weight,
        step_weight,
        step_bias.reshape(1, 64),
        decay_log,
        skip_gain.reshape(1, 64),
        scan_state,
        output_weight,
    )
    operands = [
        pltpu.with_memory_space_constraint(x, pltpu.HBM) for x in operands
    ]
    held = [pltpu.SMEM(lengths.shape, lengths.dtype)]
    held += [pltpu.VMEM(x.shape, x.dtype) for x in operands[1:]]
    scratch = [
        pltpu.VMEM((16, 2, 8, 128), F32),
        pltpu.VMEM((15, 2, 8, 128), F32),
        pltpu.VMEM((2, 8, 128), F32),
        pltpu.VMEM((7, 2, 8, 128), F32),
        pltpu.VMEM((16, 8, 128), F32),
        pltpu.VMEM((16, 4, 128), F32),
        pltpu.VMEM((16, 32, 128), BF16),
        pltpu.VMEM((5, 4, 128), F32),
        pltpu.VMEM((15, 5, 4, 128), F32),
        pltpu.VMEM((16, 128), BF16),
        pltpu.VMEM((15, 16, 128), BF16),
        pltpu.VMEM((4, 128), F32),
        pltpu.VMEM((15, 4, 128), F32),
        pltpu.VMEM((8, 32, 128), BF16),
        pltpu.VMEM((15, 32, 128), BF16),
        pltpu.VMEM((8, 4, 128), F32),
        pltpu.VMEM((15, 4, 128), F32),
        pltpu.SemaphoreType.DMA((len(operands),)),
        pltpu.SemaphoreType.DMA((11,)),
        pltpu.SemaphoreType.DMA((11,)),
    ]
    layer_out, new_state = pl.pallas_call(
        kernel,
        out_shape=(
            jax.ShapeDtypeStruct((4, 32), F32),
            jax.ShapeDtypeStruct((4, 16, 64), F32),
        ),
        in_specs=[pl.BlockSpec(memory_space=pltpu.HBM)] * len(operands),
        out_specs=(
            pl.BlockSpec(memory_space=pltpu.VMEM),
            pl.BlockSpec(memory_space=pltpu.VMEM),
        ),
        scratch_shapes=held + scratch,
        compiler_params=pltpu.CompilerParams(
            collective_id=0, has_side_effects=True, vmem_limit_bytes=24 << 20
        ),
        name="decode_step",
    )(*operands)
    return layer_out.astype(BF16), new_state


def solution(mesh):
    placed = (
        P(None, "tp", None),
        P(None, "ctx", "tp", None),
        P(None, "ctx", "tp", None),
        P(),
        P(None, "ctx"),
        P("ctx", "tp"),
        P(),
        P(("ctx", "tp"), None),
        P(("ctx", "tp"), None),
        P(None, ("ctx", "tp")),
        P(("ctx", "tp")),
        P(None, None, ("ctx", "tp")),
        P(("ctx", "tp"), None),
        P(("ctx", "tp"), None),
        P(("ctx", "tp")),
        P(None, ("ctx", "tp")),
        P(("ctx", "tp")),
        P(None, None, ("ctx", "tp")),
        P(("ctx", "tp"), None),
    )
    return jax.shard_map(
        on_device,
        mesh=mesh,
        in_specs=placed,
        out_specs=(P(None, ("ctx", "tp")), P(None, None, ("ctx", "tp"))),
        check_vma=False,
    )
```

```python
import functools

import jax
import jax.numpy as jnp
from jax import lax
from jax.experimental import pallas as pl
from jax.experimental.pallas import tpu as pltpu
from jax.sharding import PartitionSpec as P

MESH = pl.DeviceIdType.MESH
F32 = jnp.float32
BF16 = jnp.bfloat16


def far_first(n):
    return sorted(range(1, n), key=lambda d: -min(d, n - d))


def nt(left, right):
    return lax.dot_general(
        left, right, (((1,), (1,)), ((), ())), preferred_element_type=F32
    )


def silu(x):
    return x * (1.0 / (1.0 + jnp.exp(-x)))


def softplus(x):
    return jnp.maximum(x, 0.0) + jnp.log1p(jnp.exp(-jnp.abs(x)))


def iota(shape, dim):
    return lax.broadcasted_iota(jnp.int32, shape, dim)


def kernel(*refs):
    names_in = (
        "len", "q", "k", "v", "res", "gain", "iw", "gw", "cw", "cb", "cs", "pw",
        "sw", "sb", "dl", "sg", "ss", "outw",
    )
    n_in = len(names_in)
    ow = refs[n_in]
    hbm = dict(zip(names_in, refs[:n_in]))
    lo_ref, ns_ref = refs[n_in + 1 : n_in + 3]
    vm = dict(zip(names_in, refs[n_in + 3 : 2 * n_in + 3]))
    (
        obuf, r_o, ob, mlb, attf, wo, hp, r_hp, h2, p_a, r_pa, rank_b, r_rank,
        maps_b, r_maps, tb, r_t, tz, r_z, in_sem, own_sem, send_sem, recv_sem,
    ) = refs[2 * n_in + 3 :]

    c = lax.axis_index("ctx")
    h = lax.axis_index("tp")
    a = lax.div(c, 16)
    b = lax.rem(c, 16)
    z = lax.div(b, 2)
    core = lax.rem(b, 2)
    e = a * 2 + h

    def in_a8(d):
        other = lax.rem(a + d, 8)
        return other, (other * 16 + b, h)

    def in_yx(d):
        other = lax.rem(e + d, 16)
        return other, (lax.div(other, 2) * 16 + b, lax.rem(other, 2))

    def in_b16(d):
        other = lax.rem(b + d, 16)
        return other, (a * 16 + other, h)

    loads = {
        name: pltpu.make_async_copy(hbm[name], vm[name], in_sem.at[i])
        for i, name in enumerate(names_in)
    }

    def need(*names):
        for name in names:
            loads.pop(name).wait()

    first = ("k", "q", "len", "v")
    for name in first:
        loads[name].start()

    barrier = pltpu.get_barrier_semaphore()
    greeted = [in_b16(d)[1] for d in far_first(16)]
    greeted += [in_a8(d)[1] for d in far_first(8)] + [(c, 1 - h)]
    for peer in greeted:
        pl.semaphore_signal(barrier, 1, device_id=peer, device_id_type=MESH)

    def send(src, dst, stage, peer):
        pltpu.make_async_remote_copy(
            src, dst, send_sem.at[stage], recv_sem.at[stage],
            device_id=peer, device_id_type=MESH,
        ).start()

    def arrived(block, stage):
        pltpu.make_async_copy(block, block, recv_sem.at[stage]).wait()

    pending = []

    def sent(block, stage):
        pltpu.make_async_copy(block, block, send_sem.at[stage]).wait()

    shape = (32, 512)
    column = iota(shape, 1)
    same_head = lax.rem(column, 4) == lax.div(iota(shape, 0), 8)
    position = c * 128 + lax.div(column, 4)
    lane16 = iota((16, 128), 1)
    on_diag = lane16 == iota((16, 128), 0)
    low4 = iota((4, 128), 1) < 64
    need(*first)
    for r in range(4):
        scores = nt(vm["q"][r], vm["k"][r]) * (128.0 ** -0.5)
        live = jnp.logical_and(same_head, position < vm["len"][r])
        scores = jnp.where(live, scores, -1e30)
        high = jnp.max(scores, axis=1, keepdims=True)
        weights = jnp.where(live, jnp.exp(scores - high), 0.0)
        total = jnp.sum(weights, axis=1, keepdims=True)
        summed = jnp.dot(
            weights.astype(BF16), vm["v"][r], preferred_element_type=F32
        )
        for i in range(8):
            rows = slice(i * 4, i * 4 + 4)
            obuf[i, 0, r * 4 : r * 4 + 4] = summed[rows]
            obuf[i, 1, r * 4 : r * 4 + 4] = jnp.where(low4, high[rows], total[rows])

    pl.semaphore_wait(barrier, len(greeted))

    for d in far_first(8):
        other, peer = in_a8(d)
        send(obuf.at[other], r_o.at[d - 1], 0, peer)
    pending.append((r_o, 0))

    def columns_of(device):
        return ow.at[:, pl.ds(pl.multiple_of(device * 512, 512), 512)]

    mine = wo.at[pl.ds(pl.multiple_of(a * 64, 64), 64)]
    for d in far_first(8):
        other, peer = in_a8(d)
        send(columns_of(other), mine, 1, peer)
    pending.append((wo.at[pl.ds(0, 448)], 1))
    own_columns = pltpu.make_async_copy(columns_of(a), mine, own_sem)
    own_columns.start()
    for name in names_in:
        if name not in first:
            loads[name].start()

    arrived(r_o, 0)
    parts = [(obuf[a, 0], obuf[a, 1])] + [(r_o[i, 0], r_o[i, 1]) for i in range(7)]
    highs = [ml[:, 0:1] for _, ml in parts]
    totals = [ml[:, 64:65] for _, ml in parts]
    top = functools.reduce(jnp.maximum, highs)
    scales = [jnp.exp(high - top) for high in highs]
    total = sum(s * t for s, t in zip(scales, totals))
    summed = sum(s * o for s, (o, _) in zip(scales, parts))

    ob[b] = summed.astype(BF16)
    mlb[b, 0:1] = jnp.sum(jnp.where(on_diag, top, 0.0), axis=0, keepdims=True)
    mlb[b, 1:2] = jnp.sum(jnp.where(on_diag, total, 0.0), axis=0, keepdims=True)
    for d in far_first(16):
        _, peer = in_b16(d)
        send(mlb.at[b], mlb.at[b], 2, peer)
        send(ob.at[b], ob.at[b], 3, peer)
    pending.append((mlb.at[pl.ds(0, 15)], 2))
    pending.append((ob.at[pl.ds(0, 15)], 3))
    arrived(mlb.at[pl.ds(0, 15)], 2)
    high_rows = mlb[:, 0, :]
    total_rows = mlb[:, 1, :]
    scale_rows = jnp.exp(high_rows - jnp.max(high_rows, axis=0, keepdims=True))
    all_total = jnp.sum(scale_rows * total_rows, axis=0, keepdims=True)
    valid = iota((1, 128), 1) < 16
    scale_rows = scale_rows / jnp.where(valid, all_total, 1.0)
    columns = [
        jnp.sum(jnp.where(on_diag, scale_rows[i : i + 1], 0.0), axis=1, keepdims=True)
        for i in range(16)
    ]
    arrived(ob.at[pl.ds(0, 15)], 3)
    attended = sum(columns[i] * ob[i].astype(F32) for i in range(16))

    for r in range(4):
        attf[r] = attended[r * 4 : r * 4 + 4]
    flat = jnp.concatenate([attf[:, i, :] for i in range(4)], axis=1).astype(BF16)
    need("res")
    own_columns.wait()
    arrived(wo.at[pl.ds(0, 448)], 1)
    partial = nt(flat, wo[...])
    rest = vm["res"][...].astype(F32)
    twice = jnp.concatenate([rest, rest], axis=1)
    adds = jnp.logical_and(low4 == (lax.rem(a, 2) == 0), h == 0)
    rest = jnp.where(adds, twice, 0.0)
    for i in range(4):
        hp[i] = partial[:, i * 128 : i * 128 + 128] + jnp.where(
            lax.div(a, 2) == i, rest, 0.0
        )

    for d in far_first(16):
        _, peer = in_yx(d)
        send(hp, r_hp.at[d - 1], 4, peer)
    pending.append((r_hp, 4))
    arrived(r_hp, 4)
    h2[b] = (hp[...] + jnp.sum(r_hp[...], axis=0)).reshape(16, 128).astype(BF16)
    for d in far_first(16):
        _, peer = in_b16(d)
        send(h2.at[b], h2.at[b], 5, peer)
    pending.append((h2.at[pl.ds(0, 15)], 5))
    need("gain", "iw", "gw", "cw", "cb", "cs", "pw")
    conv = vm["cb"][...]
    for i in range(3):
        conv = conv + vm["cs"][i].astype(F32) * vm["cw"][i : i + 1]
    arrived(h2.at[pl.ds(0, 15)], 5)

    def swapped(x):
        return jnp.concatenate([x[:, 64:], x[:, :64]], axis=1)

    low16 = lane16 < 64
    evens, odds = [], []
    for i in range(8):
        left = h2[2 * i].astype(F32)
        right = h2[2 * i + 1].astype(F32)
        evens.append(jnp.where(low16, left, swapped(right)))
        odds.append(jnp.where(low16, swapped(left), right))
    squares = jnp.sum(sum(x * x for x in evens + odds), axis=1, keepdims=True)
    square = sum(squares[i * 4 : i * 4 + 4] for i in range(4))
    scale = lax.rsqrt(square * (1.0 / 8192.0) + 1e-5)
    gain = vm["gain"][...]
    blocks = []
    for i in range(64):
        block = (odds if i // 8 % 2 else evens)[i % 8]
        row = i // 16 * 4
        blocks.append(block[row : row + 4] * scale * gain[i : i + 1])
    normed = jnp.concatenate(blocks, axis=1).astype(BF16)
    inputs = nt(normed, vm["iw"][...])
    mixed = silu(conv + inputs * vm["cw"][3:4])

    local = jnp.dot(mixed.astype(BF16), vm["pw"][...], preferred_element_type=F32)
    for i in range(4):
        p_a[i] = local[:, i * 128 : i * 128 + 128]
    p_a[4] = jnp.concatenate([local[:, 512:544], jnp.zeros((4, 96), F32)], axis=1)
    for d in far_first(16):
        _, peer = in_yx(d)
        send(p_a, r_pa.at[d - 1], 6, peer)
    pending.append((r_pa, 6))
    gates = silu(nt(normed, vm["gw"][...]))
    need("sw", "sb", "dl", "sg", "ss", "outw")
    rate = jnp.exp(vm["dl"][...])
    skip = vm["sg"][...] * mixed
    arrived(r_pa, 6)
    projected = p_a[...] + jnp.sum(r_pa[...], axis=0)
    ranks = projected[0:4].reshape(16, 128)
    rank_b[...] = ranks.astype(BF16)
    maps_b[...] = projected[4]
    for d in far_first(16):
        _, peer = in_b16(d)
        send(rank_b, r_rank.at[d - 1], 7, peer)
        send(maps_b, r_maps.at[d - 1], 8, peer)
    pending.append((r_rank, 7))
    pending.append((r_maps, 8))
    arrived(r_rank, 7)
    ranks = ranks + jnp.sum(r_rank[...].astype(F32), axis=0)
    arrived(r_maps, 8)
    maps = maps_b[...] + jnp.sum(r_maps[...], axis=0)

    rank = jnp.concatenate(
        [ranks[i * 4 : i * 4 + 4] for i in range(4)], axis=1
    ).astype(BF16)
    step = softplus(nt(rank, vm["sw"][...]) + vm["sb"][...])
    pick_leave = lane16 == iota((16, 128), 0) + 16
    rows = []
    for r in range(4):
        row = maps[r : r + 1]
        entry = jnp.sum(jnp.where(on_diag, row, 0.0), axis=1, keepdims=True)
        leave = jnp.sum(jnp.where(pick_leave, row, 0.0), axis=1, keepdims=True)
        step_r = step[r : r + 1]
        state = jnp.exp(-step_r * rate) * vm["ss"][r] + entry * (step_r * mixed[r : r + 1])
        ns_ref[r] = state
        rows.append(jnp.sum(state * leave, axis=0, keepdims=True))
    gated = ((jnp.concatenate(rows, axis=0) + skip) * gates).astype(BF16)

    term = jnp.dot(gated, vm["outw"][...], preferred_element_type=F32)
    for i in range(8):
        tb[i] = jnp.concatenate(
            [
                term[:, (i * 8 + k) * 128 : (i * 8 + k) * 128 + 128]
                for k in range(8)
            ],
            axis=0,
        ).astype(BF16)
    for d in far_first(16):
        other, peer = in_yx(d)
        send(tb.at[lax.div(other, 2)], r_t.at[d - 1], 9, peer)
    pending.append((r_t, 9))
    near = h2[b].astype(F32)
    near = sum(
        jnp.where(lax.div(a, 2) == i, near[i * 4 : i * 4 + 4], 0.0) for i in range(4)
    )

    def quarter(block, place):
        picked = block[:, 0:32]
        for i in range(1, 4):
            picked = jnp.where(place == i, block[:, i * 32 : i * 32 + 32], picked)
        return picked

    own = quarter(near, lax.rem(a, 2) * 2 + h)
    arrived(r_t, 9)
    summed = tb[a].astype(F32) + jnp.sum(r_t[...].astype(F32), axis=0)
    tz[...] = summed.reshape(8, 4, 128)
    for d in far_first(16):
        other, peer = in_b16(d)
        send(tz.at[lax.div(other, 2)], r_z.at[d - 1], 10, peer)
    pending.append((r_z, 10))
    arrived(r_z, 10)
    whole = tz[z] + jnp.sum(r_z[...], axis=0)
    lo_ref[...] = quarter(whole, core * 2 + h) + own

    for block, stage in pending:
        sent(block, stage)


def on_device(
    query, keys, values, lengths, residual, out_weight, norm_gain, input_weight,
    gate_weight, conv_weight, conv_bias, conv_state, proj_weight, step_weight,
    step_bias, decay_log, skip_gain, scan_state, output_weight,
):
    operands = (
        lengths,
        query,
        keys.reshape(4, 512, 128),
        values.reshape(4, 512, 128),
        residual,
        norm_gain.reshape(64, 128),
        input_weight,
        gate_weight,
        conv_weight,
        conv_bias.reshape(1, 64),
        conv_state.transpose(1, 0, 2),
        proj_weight,
        step_weight,
        step_bias.reshape(1, 64),
        decay_log,
        skip_gain.reshape(1, 64),
        scan_state,
        output_weight,
    )
    held = [pltpu.SMEM(lengths.shape, lengths.dtype)]
    held += [pltpu.VMEM(x.shape, x.dtype) for x in operands[1:]]
    operands = [
        pltpu.with_memory_space_constraint(x, pltpu.HBM)
        for x in operands + (out_weight,)
    ]
    scratch = [
        pltpu.VMEM((8, 2, 16, 128), F32),
        pltpu.VMEM((7, 2, 16, 128), F32),
        pltpu.VMEM((16, 16, 128), BF16),
        pltpu.VMEM((16, 2, 128), F32),
        pltpu.VMEM((4, 4, 128), F32),
        pltpu.VMEM((512, 512), BF16),
        pltpu.VMEM((4, 4, 128), F32),
        pltpu.VMEM((15, 4, 4, 128), F32),
        pltpu.VMEM((16, 16, 128), BF16),
        pltpu.VMEM((5, 4, 128), F32),
        pltpu.VMEM((15, 5, 4, 128), F32),
        pltpu.VMEM((16, 128), BF16),
        pltpu.VMEM((15, 16, 128), BF16),
        pltpu.VMEM((4, 128), F32),
        pltpu.VMEM((15, 4, 128), F32),
        pltpu.VMEM((8, 32, 128), BF16),
        pltpu.VMEM((15, 32, 128), BF16),
        pltpu.VMEM((8, 4, 128), F32),
        pltpu.VMEM((15, 4, 128), F32),
        pltpu.SemaphoreType.DMA((len(held),)),
        pltpu.SemaphoreType.DMA,
        pltpu.SemaphoreType.DMA((11,)),
        pltpu.SemaphoreType.DMA((11,)),
    ]
    layer_out, new_state = pl.pallas_call(
        kernel,
        out_shape=(
            jax.ShapeDtypeStruct((4, 32), F32),
            jax.ShapeDtypeStruct((4, 16, 64), F32),
        ),
        in_specs=[pl.BlockSpec(memory_space=pltpu.HBM)] * len(operands),
        out_specs=(
            pl.BlockSpec(memory_space=pltpu.VMEM),
            pl.BlockSpec(memory_space=pltpu.VMEM),
        ),
        scratch_shapes=held + scratch,
        compiler_params=pltpu.CompilerParams(
            collective_id=0, has_side_effects=True, vmem_limit_bytes=24 << 20
        ),
        name="decode_step",
    )(*operands)
    return layer_out.astype(BF16), new_state


def solution(mesh):
    placed = (
        P(None, "tp", None),
        P(None, "ctx", "tp", None),
        P(None, "ctx", "tp", None),
        P(),
        P(None, "ctx"),
        P("ctx", "tp"),
        P(),
        P(("ctx", "tp"), None),
        P(("ctx", "tp"), None),
        P(None, ("ctx", "tp")),
        P(("ctx", "tp")),
        P(None, None, ("ctx", "tp")),
        P(("ctx", "tp"), None),
        P(("ctx", "tp"), None),
        P(("ctx", "tp")),
        P(None, ("ctx", "tp")),
        P(("ctx", "tp")),
        P(None, None, ("ctx", "tp")),
        P(("ctx", "tp"), None),
    )
    return jax.shard_map(
        on_device,
        mesh=mesh,
        in_specs=placed,
        out_specs=(P(None, ("ctx", "tp")), P(None, None, ("ctx", "tp"))),
        check_vma=False,
    )
```

```python
import functools

import jax
import jax.numpy as jnp
from jax import lax
from jax.experimental import pallas as pl
from jax.experimental.pallas import tpu as pltpu
from jax.sharding import PartitionSpec as P

MESH = pl.DeviceIdType.MESH
F32 = jnp.float32
BF16 = jnp.bfloat16


def far_first(n):
    return sorted(range(1, n), key=lambda d: -min(d, n - d))


def nt(left, right):
    return lax.dot_general(
        left, right, (((1,), (1,)), ((), ())), preferred_element_type=F32
    )


def silu(x):
    return x * (1.0 / (1.0 + jnp.exp(-x)))


def softplus(x):
    return jnp.maximum(x, 0.0) + jnp.log1p(jnp.exp(-jnp.abs(x)))


def iota(shape, dim):
    return lax.broadcasted_iota(jnp.int32, shape, dim)


def kernel(*refs):
    names_in = (
        "len", "q", "k", "v", "res", "gain", "iw", "gw", "cw", "cb", "cs", "pw",
        "sw", "sb", "dl", "sg", "ss", "outw",
    )
    n_in = len(names_in)
    ow = refs[n_in]
    hbm = dict(zip(names_in, refs[:n_in]))
    lo_ref, ns_ref = refs[n_in + 1 : n_in + 3]
    vm = dict(zip(names_in, refs[n_in + 3 : 2 * n_in + 3]))
    (
        obuf, r_o, ob, mlb, attf, wo, hp, r_hp, h2, p_a, r_pa, rank_b, r_rank,
        maps_b, r_maps, tb, r_t, tz, r_z, in_sem, own_sem, chip_sem, send_sem, recv_sem,
    ) = refs[2 * n_in + 3 :]

    c = lax.axis_index("ctx")
    h = lax.axis_index("tp")
    a = lax.div(c, 16)
    b = lax.rem(c, 16)
    z = lax.div(b, 2)
    core = lax.rem(b, 2)
    e = a * 2 + h

    def in_a8(d):
        other = lax.rem(a + d, 8)
        return other, (other * 16 + b, h)

    def in_yx(d):
        other = lax.rem(e + d, 16)
        return other, (lax.div(other, 2) * 16 + b, lax.rem(other, 2))

    def in_b16(d):
        other = lax.rem(b + d, 16)
        return other, (a * 16 + other, h)

    loads = {
        name: pltpu.make_async_copy(hbm[name], vm[name], in_sem.at[i])
        for i, name in enumerate(names_in)
    }

    def need(*names):
        for name in names:
            loads.pop(name).wait()

    first = ("k", "q", "len", "v")
    for name in first:
        loads[name].start()

    barrier = pltpu.get_barrier_semaphore()
    greeted = [in_b16(d)[1] for d in far_first(16)]
    greeted += [in_a8(d)[1] for d in far_first(8)] + [(c, 1 - h)]
    for peer in greeted:
        pl.semaphore_signal(barrier, 1, device_id=peer, device_id_type=MESH)

    def send(src, dst, stage, peer):
        pltpu.make_async_remote_copy(
            src, dst, send_sem.at[stage], recv_sem.at[stage],
            device_id=peer, device_id_type=MESH,
        ).start()

    def arrived(block, stage):
        pltpu.make_async_copy(block, block, recv_sem.at[stage]).wait()

    pending = []

    def sent(block, stage):
        pltpu.make_async_copy(block, block, send_sem.at[stage]).wait()

    shape = (32, 512)
    column = iota(shape, 1)
    same_head = lax.rem(column, 4) == lax.div(iota(shape, 0), 8)
    position = c * 128 + lax.div(column, 4)
    lane16 = iota((16, 128), 1)
    on_diag = lane16 == iota((16, 128), 0)
    low4 = iota((4, 128), 1) < 64
    need(*first)
    for r in range(4):
        scores = nt(vm["q"][r], vm["k"][r]) * (128.0 ** -0.5)
        live = jnp.logical_and(same_head, position < vm["len"][r])
        scores = jnp.where(live, scores, -1e30)
        high = jnp.max(scores, axis=1, keepdims=True)
        weights = jnp.where(live, jnp.exp(scores - high), 0.0)
        total = jnp.sum(weights, axis=1, keepdims=True)
        summed = jnp.dot(
            weights.astype(BF16), vm["v"][r], preferred_element_type=F32
        )
        for i in range(8):
            rows = slice(i * 4, i * 4 + 4)
            obuf[i, 0, r * 4 : r * 4 + 4] = summed[rows]
            obuf[i, 1, r * 4 : r * 4 + 4] = jnp.where(low4, high[rows], total[rows])

    pl.semaphore_wait(barrier, len(greeted))

    for d in far_first(8):
        other, peer = in_a8(d)
        send(obuf.at[other], r_o.at[d - 1], 0, peer)
    sent(r_o, 0)

    def columns_of(device):
        return ow.at[:, pl.ds(pl.multiple_of(device * 512, 512), 512)]

    mine = wo.at[pl.ds(pl.multiple_of(a * 64, 64), 64)]
    for d in far_first(8):
        other, peer = in_a8(d)
        send(columns_of(other), mine, 1, peer)
    pending.append((wo.at[pl.ds(0, 448)], 1))
    own_columns = pltpu.make_async_copy(columns_of(a), mine, own_sem)
    own_columns.start()
    for name in names_in:
        if name not in first:
            loads[name].start()

    arrived(r_o, 0)
    low16 = lane16 < 64

    def swapped(x):
        return jnp.concatenate([x[:, 64:], x[:, :64]], axis=1)

    outs = [obuf[a, 0]] + [r_o[i, 0] for i in range(7)]
    marks = [obuf[a, 1]] + [r_o[i, 1] for i in range(7)]
    highs = [jnp.where(low16, x, swapped(x)) for x in marks]
    top = functools.reduce(jnp.maximum, highs)
    scales = [jnp.exp(x - top) for x in highs]
    total = sum(s * x for s, x in zip(scales, marks))
    summed = sum(s * x for s, x in zip(scales, outs))

    ob[b] = summed.astype(BF16)
    packed = jnp.where(low16, top, total)
    both = jnp.logical_or(on_diag, lane16 == iota((16, 128), 0) + 64)
    mlb[b] = jnp.sum(jnp.where(both, packed, 0.0), axis=0, keepdims=True)
    for d in far_first(16):
        _, peer = in_b16(d)
        send(mlb.at[b], mlb.at[b], 2, peer)
        send(ob.at[b], ob.at[b], 3, peer)
    pending.append((mlb.at[pl.ds(0, 15)], 2))
    pending.append((ob.at[pl.ds(0, 15)], 3))
    arrived(mlb.at[pl.ds(0, 15)], 2)
    high_rows = mlb[:, 0, :]
    total_rows = swapped(high_rows)
    scale_rows = jnp.exp(high_rows - jnp.max(high_rows, axis=0, keepdims=True))
    all_total = jnp.sum(scale_rows * total_rows, axis=0, keepdims=True)
    valid = iota((1, 128), 1) < 16
    scale_rows = scale_rows / jnp.where(valid, all_total, 1.0)
    columns = [
        jnp.sum(jnp.where(on_diag, scale_rows[i : i + 1], 0.0), axis=1, keepdims=True)
        for i in range(16)
    ]
    arrived(ob.at[pl.ds(0, 15)], 3)
    attended = sum(columns[i] * ob[i].astype(F32) for i in range(16))

    for r in range(4):
        attf[r] = attended[r * 4 : r * 4 + 4]
    flat = jnp.concatenate([attf[:, i, :] for i in range(4)], axis=1).astype(BF16)
    need("res")
    own_columns.wait()
    arrived(wo.at[pl.ds(0, 448)], 1)
    partial = nt(flat, wo[...])
    rest = vm["res"][...].astype(F32)
    twice = jnp.concatenate([rest, rest], axis=1)
    adds = jnp.logical_and(low4 == (lax.rem(a, 2) == 0), h == 0)
    rest = jnp.where(adds, twice, 0.0)
    for i in range(4):
        hp[i] = partial[:, i * 128 : i * 128 + 128] + jnp.where(
            lax.div(a, 2) == i, rest, 0.0
        )

    for d in far_first(16):
        _, peer = in_yx(d)
        send(hp, r_hp.at[d - 1], 4, peer)
    pending.append((r_hp, 4))
    arrived(r_hp, 4)
    h2[b] = (hp[...] + jnp.sum(r_hp[...], axis=0)).reshape(16, 128).astype(BF16)
    for d in far_first(16):
        _, peer = in_b16(d)
        pltpu.make_async_remote_copy(
            h2.at[b], h2.at[b], send_sem.at[5], chip_sem.at[b],
            device_id=peer, device_id_type=MESH,
        ).start()
    pending.append((h2.at[pl.ds(0, 15)], 5))
    need("gain", "iw", "gw", "cw", "cb", "cs", "pw")
    conv = vm["cb"][...]
    for i in range(3):
        conv = conv + vm["cs"][i].astype(F32) * vm["cw"][i : i + 1]

    squares = jnp.zeros((16, 128), F32)
    inputs = jnp.zeros((4, 64), F32)
    gates = jnp.zeros((4, 64), F32)
    for d in (0, 1, 7, 2, 6, 3, 5, 4):
        chip = lax.rem(z + d, 8)
        awaited = [chip * 2 + core, chip * 2 + 1 - core] if d else [b + 1 - 2 * core]
        for slot in awaited:
            pltpu.make_async_copy(h2.at[slot], h2.at[slot], chip_sem.at[slot]).wait()
        left = h2[2 * chip].astype(F32)
        right = h2[2 * chip + 1].astype(F32)
        even = jnp.where(low16, left, swapped(right))
        odd = jnp.where(low16, swapped(left), right)
        squares = squares + (even * even + odd * odd)
        block = jnp.concatenate(
            [
                (odd if i % 2 else even)[i // 2 * 4 : i // 2 * 4 + 4]
                * vm["gain"][i * 8 + chip]
                for i in range(8)
            ],
            axis=1,
        ).astype(BF16)

        def times(weight):
            part = [
                weight[:, pl.ds(pl.multiple_of(i * 1024 + chip * 128, 128), 128)]
                for i in range(8)
            ]
            return nt(block, jnp.concatenate(part, axis=1))

        inputs = inputs + times(vm["iw"])
        gates = gates + times(vm["gw"])
    squares = jnp.sum(squares, axis=1, keepdims=True)
    square = sum(squares[i * 4 : i * 4 + 4] for i in range(4))
    scale = lax.rsqrt(square * (1.0 / 8192.0) + 1e-5)
    inputs = inputs * scale
    mixed = silu(conv + inputs * vm["cw"][3:4])

    local = jnp.dot(mixed.astype(BF16), vm["pw"][...], preferred_element_type=F32)
    for i in range(4):
        p_a[i] = local[:, i * 128 : i * 128 + 128]
    p_a[4] = jnp.concatenate([local[:, 512:544], jnp.zeros((4, 96), F32)], axis=1)
    for d in far_first(16):
        _, peer = in_yx(d)
        send(p_a, r_pa.at[d - 1], 6, peer)
    pending.append((r_pa, 6))
    gates = silu(gates * scale)
    need("sw", "sb", "dl", "sg", "ss", "outw")
    rate = jnp.exp(vm["dl"][...])
    skip = vm["sg"][...] * mixed
    arrived(r_pa, 6)
    projected = p_a[...] + jnp.sum(r_pa[...], axis=0)
    ranks = projected[0:4].reshape(16, 128)
    rank_b[...] = ranks.astype(BF16)
    maps_b[...] = projected[4]
    for d in far_first(16):
        _, peer = in_b16(d)
        send(rank_b, r_rank.at[d - 1], 7, peer)
        send(maps_b, r_maps.at[d - 1], 8, peer)
    pending.append((r_rank, 7))
    pending.append((r_maps, 8))
    arrived(r_rank, 7)
    ranks = ranks + jnp.sum(r_rank[...].astype(F32), axis=0)
    arrived(r_maps, 8)
    maps = maps_b[...] + jnp.sum(r_maps[...], axis=0)

    rank = jnp.concatenate(
        [ranks[i * 4 : i * 4 + 4] for i in range(4)], axis=1
    ).astype(BF16)
    step = softplus(nt(rank, vm["sw"][...]) + vm["sb"][...])
    pick_leave = lane16 == iota((16, 128), 0) + 16
    rows = []
    for r in range(4):
        row = maps[r : r + 1]
        entry = jnp.sum(jnp.where(on_diag, row, 0.0), axis=1, keepdims=True)
        leave = jnp.sum(jnp.where(pick_leave, row, 0.0), axis=1, keepdims=True)
        step_r = step[r : r + 1]
        state = jnp.exp(-step_r * rate) * vm["ss"][r] + entry * (step_r * mixed[r : r + 1])
        ns_ref[r] = state
        rows.append(jnp.sum(state * leave, axis=0, keepdims=True))
    gated = ((jnp.concatenate(rows, axis=0) + skip) * gates).astype(BF16)

    term = jnp.dot(gated, vm["outw"][...], preferred_element_type=F32)
    for i in range(8):
        tb[i] = jnp.concatenate(
            [
                term[:, (i * 8 + k) * 128 : (i * 8 + k) * 128 + 128]
                for k in range(8)
            ],
            axis=0,
        ).astype(BF16)
    for d in far_first(16):
        other, peer = in_yx(d)
        send(tb.at[lax.div(other, 2)], r_t.at[d - 1], 9, peer)
    pending.append((r_t, 9))
    near = h2[b].astype(F32)
    near = sum(
        jnp.where(lax.div(a, 2) == i, near[i * 4 : i * 4 + 4], 0.0) for i in range(4)
    )

    def quarter(block, place):
        picked = block[:, 0:32]
        for i in range(1, 4):
            picked = jnp.where(place == i, block[:, i * 32 : i * 32 + 32], picked)
        return picked

    own = quarter(near, lax.rem(a, 2) * 2 + h)
    arrived(r_t, 9)
    summed = tb[a].astype(F32) + jnp.sum(r_t[...].astype(F32), axis=0)
    tz[...] = summed.reshape(8, 4, 128)
    for d in far_first(16):
        other, peer = in_b16(d)
        send(tz.at[lax.div(other, 2)], r_z.at[d - 1], 10, peer)
    pending.append((r_z, 10))
    arrived(r_z, 10)
    whole = tz[z] + jnp.sum(r_z[...], axis=0)
    lo_ref[...] = quarter(whole, core * 2 + h) + own

    for block, stage in pending:
        sent(block, stage)


def on_device(
    query, keys, values, lengths, residual, out_weight, norm_gain, input_weight,
    gate_weight, conv_weight, conv_bias, conv_state, proj_weight, step_weight,
    step_bias, decay_log, skip_gain, scan_state, output_weight,
):
    operands = (
        lengths,
        query,
        keys.reshape(4, 512, 128),
        values.reshape(4, 512, 128),
        residual,
        norm_gain.reshape(64, 1, 128),
        input_weight,
        gate_weight,
        conv_weight,
        conv_bias.reshape(1, 64),
        conv_state.transpose(1, 0, 2),
        proj_weight,
        step_weight,
        step_bias.reshape(1, 64),
        decay_log,
        skip_gain.reshape(1, 64),
        scan_state,
        output_weight,
    )
    held = [pltpu.SMEM(lengths.shape, lengths.dtype)]
    held += [pltpu.VMEM(x.shape, x.dtype) for x in operands[1:]]
    operands = [
        pltpu.with_memory_space_constraint(x, pltpu.HBM)
        for x in operands + (out_weight,)
    ]
    scratch = [
        pltpu.VMEM((8, 2, 16, 128), F32),
        pltpu.VMEM((7, 2, 16, 128), F32),
        pltpu.VMEM((16, 16, 128), BF16),
        pltpu.VMEM((16, 1, 128), F32),
        pltpu.VMEM((4, 4, 128), F32),
        pltpu.VMEM((512, 512), BF16),
        pltpu.VMEM((4, 4, 128), F32),
        pltpu.VMEM((15, 4, 4, 128), F32),
        pltpu.VMEM((16, 16, 128), BF16),
        pltpu.VMEM((5, 4, 128), F32),
        pltpu.VMEM((15, 5, 4, 128), F32),
        pltpu.VMEM((16, 128), BF16),
        pltpu.VMEM((15, 16, 128), BF16),
        pltpu.VMEM((4, 128), F32),
        pltpu.VMEM((15, 4, 128), F32),
        pltpu.VMEM((8, 32, 128), BF16),
        pltpu.VMEM((15, 32, 128), BF16),
        pltpu.VMEM((8, 4, 128), F32),
        pltpu.VMEM((15, 4, 128), F32),
        pltpu.SemaphoreType.DMA((len(held),)),
        pltpu.SemaphoreType.DMA,
        pltpu.SemaphoreType.DMA((16,)),
        pltpu.SemaphoreType.DMA((11,)),
        pltpu.SemaphoreType.DMA((11,)),
    ]
    layer_out, new_state = pl.pallas_call(
        kernel,
        out_shape=(
            jax.ShapeDtypeStruct((4, 32), F32),
            jax.ShapeDtypeStruct((4, 16, 64), F32),
        ),
        in_specs=[pl.BlockSpec(memory_space=pltpu.HBM)] * len(operands),
        out_specs=(
            pl.BlockSpec(memory_space=pltpu.VMEM),
            pl.BlockSpec(memory_space=pltpu.VMEM),
        ),
        scratch_shapes=held + scratch,
        compiler_params=pltpu.CompilerParams(
            collective_id=0, has_side_effects=True, vmem_limit_bytes=24 << 20
        ),
        name="decode_step",
    )(*operands)
    return layer_out.astype(BF16), new_state


def solution(mesh):
    placed = (
        P(None, "tp", None),
        P(None, "ctx", "tp", None),
        P(None, "ctx", "tp", None),
        P(),
        P(None, "ctx"),
        P("ctx", "tp"),
        P(),
        P(("ctx", "tp"), None),
        P(("ctx", "tp"), None),
        P(None, ("ctx", "tp")),
        P(("ctx", "tp")),
        P(None, None, ("ctx", "tp")),
        P(("ctx", "tp"), None),
        P(("ctx", "tp"), None),
        P(("ctx", "tp")),
        P(None, ("ctx", "tp")),
        P(("ctx", "tp")),
        P(None, None, ("ctx", "tp")),
        P(("ctx", "tp"), None),
    )
    return jax.shard_map(
        on_device,
        mesh=mesh,
        in_specs=placed,
        out_specs=(P(None, ("ctx", "tp")), P(None, None, ("ctx", "tp"))),
        check_vma=False,
    )
```

```python
import functools

import jax
import jax.numpy as jnp
from jax import lax
from jax.experimental import pallas as pl
from jax.experimental.pallas import tpu as pltpu
from jax.sharding import PartitionSpec as P

MESH = pl.DeviceIdType.MESH
F32 = jnp.float32
BF16 = jnp.bfloat16


def far_first(n):
    return sorted(range(1, n), key=lambda d: -min(d, n - d))


def nt(left, right):
    return lax.dot_general(
        left, right, (((1,), (1,)), ((), ())), preferred_element_type=F32
    )


def silu(x):
    return x * (1.0 / (1.0 + jnp.exp(-x)))


def softplus(x):
    return jnp.maximum(x, 0.0) + jnp.log1p(jnp.exp(-jnp.abs(x)))


def iota(shape, dim):
    return lax.broadcasted_iota(jnp.int32, shape, dim)


def kernel(*refs):
    names_in = (
        "len", "q", "k", "v", "res", "gain", "iw", "gw", "cw", "cb", "cs", "pw",
        "sw", "sb", "dl", "sg", "ss", "outw",
    )
    n_in = len(names_in)
    ow = refs[n_in]
    hbm = dict(zip(names_in, refs[:n_in]))
    lo_ref, ns_ref = refs[n_in + 1 : n_in + 3]
    vm = dict(zip(names_in, refs[n_in + 3 : 2 * n_in + 3]))
    (
        obuf, r_o, ob, mlb, attf, wo, hp, r_hp, h2, p_a, r_pa, rank_b, r_rank,
        maps_b, r_maps, tb, td, r_d, in_sem, own_sem, chip_sem, send_sem, recv_sem,
    ) = refs[2 * n_in + 3 :]

    c = lax.axis_index("ctx")
    h = lax.axis_index("tp")
    a = lax.div(c, 16)
    b = lax.rem(c, 16)
    z = lax.div(b, 2)
    core = lax.rem(b, 2)
    e = a * 2 + h

    def in_a8(d):
        other = lax.rem(a + d, 8)
        return other, (other * 16 + b, h)

    def in_yx(d):
        other = lax.rem(e + d, 16)
        return other, (lax.div(other, 2) * 16 + b, lax.rem(other, 2))

    def in_b16(d):
        other = lax.rem(b + d, 16)
        return other, (a * 16 + other, h)

    loads = {
        name: pltpu.make_async_copy(hbm[name], vm[name], in_sem.at[i])
        for i, name in enumerate(names_in)
    }

    def need(*names):
        for name in names:
            loads.pop(name).wait()

    barrier = pltpu.get_barrier_semaphore()
    greeted = [in_b16(d)[1] for d in far_first(16)]
    greeted += [in_a8(d)[1] for d in far_first(8)] + [(c, 1 - h)]
    for peer in greeted:
        pl.semaphore_signal(barrier, 1, device_id=peer, device_id_type=MESH)

    first = ("k", "q", "len", "v")
    for name in first:
        loads[name].start()


    def send(src, dst, stage, peer):
        pltpu.make_async_remote_copy(
            src, dst, send_sem.at[stage], recv_sem.at[stage],
            device_id=peer, device_id_type=MESH,
        ).start()

    def arrived(block, stage):
        pltpu.make_async_copy(block, block, recv_sem.at[stage]).wait()

    pending = []

    def sent(block, stage):
        pltpu.make_async_copy(block, block, send_sem.at[stage]).wait()

    shape = (32, 512)
    column = iota(shape, 1)
    same_head = lax.rem(column, 4) == lax.div(iota(shape, 0), 8)
    position = c * 128 + lax.div(column, 4)
    lane16 = iota((16, 128), 1)
    on_diag = lane16 == iota((16, 128), 0)
    low4 = iota((4, 128), 1) < 64
    need(*first)
    for r in range(4):
        scores = nt(vm["q"][r], vm["k"][r]) * (128.0 ** -0.5)
        live = jnp.logical_and(same_head, position < vm["len"][r])
        scores = jnp.where(live, scores, -1e30)
        high = jnp.max(scores, axis=1, keepdims=True)
        weights = jnp.where(live, jnp.exp(scores - high), 0.0)
        total = jnp.sum(weights, axis=1, keepdims=True)
        summed = jnp.dot(
            weights.astype(BF16), vm["v"][r], preferred_element_type=F32
        )
        for i in range(8):
            rows = slice(i * 4, i * 4 + 4)
            obuf[i, 0, r * 4 : r * 4 + 4] = summed[rows]
            obuf[i, 1, r * 4 : r * 4 + 4] = jnp.where(low4, high[rows], total[rows])

    pl.semaphore_wait(barrier, len(greeted))

    for d in far_first(8):
        other, peer = in_a8(d)
        send(obuf.at[other], r_o.at[d - 1], 0, peer)
    sent(r_o, 0)

    def columns_of(device):
        return ow.at[:, pl.ds(pl.multiple_of(device * 512, 512), 512)]

    mine = wo.at[pl.ds(pl.multiple_of(a * 64, 64), 64)]
    for d in far_first(8):
        other, peer = in_a8(d)
        send(columns_of(other), mine, 1, peer)
    pending.append((wo.at[pl.ds(0, 448)], 1))
    own_columns = pltpu.make_async_copy(columns_of(a), mine, own_sem)
    own_columns.start()
    for name in names_in:
        if name not in first:
            loads[name].start()

    arrived(r_o, 0)
    low16 = lane16 < 64

    def swapped(x):
        return jnp.concatenate([x[:, 64:], x[:, :64]], axis=1)

    outs = [obuf[a, 0]] + [r_o[i, 0] for i in range(7)]
    marks = [obuf[a, 1]] + [r_o[i, 1] for i in range(7)]
    highs = [jnp.where(low16, x, swapped(x)) for x in marks]
    top = functools.reduce(jnp.maximum, highs)
    scales = [jnp.exp(x - top) for x in highs]
    total = sum(s * x for s, x in zip(scales, marks))
    summed = sum(s * x for s, x in zip(scales, outs))

    ob[b] = summed.astype(BF16)
    packed = jnp.where(low16, top, total)
    both = jnp.logical_or(on_diag, lane16 == iota((16, 128), 0) + 64)
    mlb[b] = jnp.sum(jnp.where(both, packed, 0.0), axis=0, keepdims=True)
    for d in far_first(16):
        _, peer = in_b16(d)
        send(mlb.at[b], mlb.at[b], 2, peer)
        send(ob.at[b], ob.at[b], 3, peer)
    pending.append((mlb.at[pl.ds(0, 15)], 2))
    pending.append((ob.at[pl.ds(0, 15)], 3))
    arrived(mlb.at[pl.ds(0, 15)], 2)
    high_rows = mlb[:, 0, :]
    total_rows = swapped(high_rows)
    scale_rows = jnp.exp(high_rows - jnp.max(high_rows, axis=0, keepdims=True))
    all_total = jnp.sum(scale_rows * total_rows, axis=0, keepdims=True)
    valid = iota((1, 128), 1) < 16
    scale_rows = scale_rows / jnp.where(valid, all_total, 1.0)
    columns = [
        jnp.sum(jnp.where(on_diag, scale_rows[i : i + 1], 0.0), axis=1, keepdims=True)
        for i in range(16)
    ]
    arrived(ob.at[pl.ds(0, 15)], 3)
    attended = sum(columns[i] * ob[i].astype(F32) for i in range(16))

    for r in range(4):
        attf[r] = attended[r * 4 : r * 4 + 4]
    flat = jnp.concatenate([attf[:, i, :] for i in range(4)], axis=1).astype(BF16)
    need("res")
    own_columns.wait()
    arrived(wo.at[pl.ds(0, 448)], 1)
    partial = nt(flat, wo[...])
    rest = vm["res"][...].astype(F32)
    twice = jnp.concatenate([rest, rest], axis=1)
    adds = jnp.logical_and(low4 == (lax.rem(a, 2) == 0), h == 0)
    rest = jnp.where(adds, twice, 0.0)
    for i in range(4):
        hp[i] = partial[:, i * 128 : i * 128 + 128] + jnp.where(
            lax.div(a, 2) == i, rest, 0.0
        )

    for d in far_first(16):
        _, peer = in_yx(d)
        send(hp, r_hp.at[d - 1], 4, peer)
    pending.append((r_hp, 4))
    arrived(r_hp, 4)
    h2[b] = (hp[...] + jnp.sum(r_hp[...], axis=0)).reshape(16, 128).astype(BF16)
    for d in far_first(16):
        _, peer = in_b16(d)
        pltpu.make_async_remote_copy(
            h2.at[b], h2.at[b], send_sem.at[5], chip_sem.at[b],
            device_id=peer, device_id_type=MESH,
        ).start()
    pending.append((h2.at[pl.ds(0, 15)], 5))
    need("gain", "iw", "gw", "cw", "cb", "cs", "pw")
    conv = vm["cb"][...]
    for i in range(3):
        conv = conv + vm["cs"][i].astype(F32) * vm["cw"][i : i + 1]

    squares = jnp.zeros((16, 128), F32)
    inputs = jnp.zeros((4, 64), F32)
    gates = jnp.zeros((4, 64), F32)
    for d in (0, 1, 7, 2, 6, 3, 5, 4):
        chip = lax.rem(z + d, 8)
        awaited = [chip * 2 + core, chip * 2 + 1 - core] if d else [b + 1 - 2 * core]
        for slot in awaited:
            pltpu.make_async_copy(h2.at[slot], h2.at[slot], chip_sem.at[slot]).wait()
        left = h2[2 * chip].astype(F32)
        right = h2[2 * chip + 1].astype(F32)
        even = jnp.where(low16, left, swapped(right))
        odd = jnp.where(low16, swapped(left), right)
        squares = squares + (even * even + odd * odd)
        block = jnp.concatenate(
            [
                (odd if i % 2 else even)[i // 2 * 4 : i // 2 * 4 + 4]
                * vm["gain"][i * 8 + chip]
                for i in range(8)
            ],
            axis=1,
        ).astype(BF16)

        def times(weight):
            part = [
                weight[:, pl.ds(pl.multiple_of(i * 1024 + chip * 128, 128), 128)]
                for i in range(8)
            ]
            return nt(block, jnp.concatenate(part, axis=1))

        inputs = inputs + times(vm["iw"])
        gates = gates + times(vm["gw"])
    squares = jnp.sum(squares, axis=1, keepdims=True)
    square = sum(squares[i * 4 : i * 4 + 4] for i in range(4))
    scale = lax.rsqrt(square * (1.0 / 8192.0) + 1e-5)
    inputs = inputs * scale
    mixed = silu(conv + inputs * vm["cw"][3:4])

    local = jnp.dot(mixed.astype(BF16), vm["pw"][...], preferred_element_type=F32)
    for i in range(4):
        p_a[i] = local[:, i * 128 : i * 128 + 128]
    p_a[4] = jnp.concatenate([local[:, 512:544], jnp.zeros((4, 96), F32)], axis=1)
    for d in far_first(16):
        _, peer = in_yx(d)
        send(p_a, r_pa.at[d - 1], 6, peer)
    pending.append((r_pa, 6))
    gates = silu(gates * scale)
    need("sw", "sb", "dl", "sg", "ss", "outw")
    rate = jnp.exp(vm["dl"][...])
    skip = vm["sg"][...] * mixed
    arrived(r_pa, 6)
    projected = p_a[...] + jnp.sum(r_pa[...], axis=0)
    ranks = projected[0:4].reshape(16, 128)
    rank_b[...] = ranks.astype(BF16)
    maps_b[...] = projected[4]
    for d in far_first(16):
        _, peer = in_b16(d)
        send(rank_b, r_rank.at[d - 1], 7, peer)
        send(maps_b, r_maps.at[d - 1], 8, peer)
    pending.append((r_rank, 7))
    pending.append((r_maps, 8))
    arrived(r_rank, 7)
    ranks = ranks + jnp.sum(r_rank[...].astype(F32), axis=0)
    arrived(r_maps, 8)
    maps = maps_b[...] + jnp.sum(r_maps[...], axis=0)

    rank = jnp.concatenate(
        [ranks[i * 4 : i * 4 + 4] for i in range(4)], axis=1
    ).astype(BF16)
    step = softplus(nt(rank, vm["sw"][...]) + vm["sb"][...])
    pick_leave = lane16 == iota((16, 128), 0) + 16
    rows = []
    for r in range(4):
        row = maps[r : r + 1]
        entry = jnp.sum(jnp.where(on_diag, row, 0.0), axis=1, keepdims=True)
        leave = jnp.sum(jnp.where(pick_leave, row, 0.0), axis=1, keepdims=True)
        step_r = step[r : r + 1]
        state = jnp.exp(-step_r * rate) * vm["ss"][r] + entry * (step_r * mixed[r : r + 1])
        ns_ref[r] = state
        rows.append(jnp.sum(state * leave, axis=0, keepdims=True))
    gated = ((jnp.concatenate(rows, axis=0) + skip) * gates).astype(BF16)

    term = jnp.dot(gated, vm["outw"][...], preferred_element_type=F32)
    for i in range(64):
        tb[i] = term[:, i * 128 : i * 128 + 128]
    group = lax.div(iota((64, 128), 1), 32)
    spread = [tb[:, r, :] for r in range(4)]
    for q in range(4):
        shares = jnp.zeros((64, 128), F32)
        for r in range(4):
            turn = (q - r) % 4 * 32
            x = spread[r]
            if turn:
                x = jnp.concatenate([x[:, turn:], x[:, :turn]], axis=1)
            shares = jnp.where(group == r, x, shares)
        td[q] = shares.reshape(64, 1, 128)
    offsets = [
        (dy, dx, dz, dc, dh)
        for dy in range(4)
        for dx in range(2)
        for dz in range(8)
        for dc in range(2)
        for dh in range(2)
    ]

    def hops(offset):
        dy, dx, dz, dc, dh = offset
        across = (0, 1, 2, 1)[dh * 2 + dx]
        return min(dy, 4 - dy) + across + min(dz, 8 - dz) + 1.5 * dc

    offsets = sorted(offsets[1:], key=lambda o: -hops(o))
    y, xl = lax.div(a, 2), lax.rem(a, 2)
    rows_of = {
        (dy, dx): lax.rem(y + dy, 4) * 2 + (1 - xl if dx else xl)
        for dy in range(4)
        for dx in range(2)
    }
    rings = [lax.rem(z + dz, 8) for dz in range(8)]
    cores = (core, 1 - core)
    sides = (h, 1 - h)
    for slot, (dy, dx, dz, dc, dh) in enumerate(offsets):
        row, ring = rows_of[dy, dx], rings[dz]
        send(
            td.at[cores[dc] * 2 + sides[dh], row * 8 + ring], r_d.at[slot], 9,
            (row * 16 + ring * 2 + cores[dc], sides[dh]),
        )
    pending.append((r_d, 9))
    near = h2[b].astype(F32)
    near = sum(
        jnp.where(lax.div(a, 2) == i, near[i * 4 : i * 4 + 4], 0.0) for i in range(4)
    )
    place = lax.rem(a, 2) * 2 + h
    own = near[:, 0:32]
    for i in range(1, 4):
        own = jnp.where(place == i, near[:, i * 32 : i * 32 + 32], own)
    arrived(r_d, 9)
    whole = td[core * 2 + h, a * 8 + z] + jnp.sum(r_d[...], axis=0)
    for r in range(4):
        lo_ref[r : r + 1] = whole[:, r * 32 : r * 32 + 32] + own[r : r + 1]

    for block, stage in pending:
        sent(block, stage)


def on_device(
    query, keys, values, lengths, residual, out_weight, norm_gain, input_weight,
    gate_weight, conv_weight, conv_bias, conv_state, proj_weight, step_weight,
    step_bias, decay_log, skip_gain, scan_state, output_weight,
):
    operands = (
        lengths,
        query,
        keys.reshape(4, 512, 128),
        values.reshape(4, 512, 128),
        residual,
        norm_gain.reshape(64, 1, 128),
        input_weight,
        gate_weight,
        conv_weight,
        conv_bias.reshape(1, 64),
        conv_state.transpose(1, 0, 2),
        proj_weight,
        step_weight,
        step_bias.reshape(1, 64),
        decay_log,
        skip_gain.reshape(1, 64),
        scan_state,
        output_weight,
    )
    held = [pltpu.SMEM(lengths.shape, lengths.dtype)]
    held += [pltpu.VMEM(x.shape, x.dtype) for x in operands[1:]]
    operands = [
        pltpu.with_memory_space_constraint(x, pltpu.HBM)
        for x in operands + (out_weight,)
    ]
    scratch = [
        pltpu.VMEM((8, 2, 16, 128), F32),
        pltpu.VMEM((7, 2, 16, 128), F32),
        pltpu.VMEM((16, 16, 128), BF16),
        pltpu.VMEM((16, 1, 128), F32),
        pltpu.VMEM((4, 4, 128), F32),
        pltpu.VMEM((512, 512), BF16),
        pltpu.VMEM((4, 4, 128), F32),
        pltpu.VMEM((15, 4, 4, 128), F32),
        pltpu.VMEM((16, 16, 128), BF16),
        pltpu.VMEM((5, 4, 128), F32),
        pltpu.VMEM((15, 5, 4, 128), F32),
        pltpu.VMEM((16, 128), BF16),
        pltpu.VMEM((15, 16, 128), BF16),
        pltpu.VMEM((4, 128), F32),
        pltpu.VMEM((15, 4, 128), F32),
        pltpu.VMEM((64, 4, 128), F32),
        pltpu.VMEM((4, 64, 1, 128), F32),
        pltpu.VMEM((255, 1, 128), F32),
        pltpu.SemaphoreType.DMA((len(held),)),
        pltpu.SemaphoreType.DMA,
        pltpu.SemaphoreType.DMA((16,)),
        pltpu.SemaphoreType.DMA((11,)),
        pltpu.SemaphoreType.DMA((11,)),
    ]
    layer_out, new_state = pl.pallas_call(
        kernel,
        out_shape=(
            jax.ShapeDtypeStruct((4, 32), F32),
            jax.ShapeDtypeStruct((4, 16, 64), F32),
        ),
        in_specs=[pl.BlockSpec(memory_space=pltpu.HBM)] * len(operands),
        out_specs=(
            pl.BlockSpec(memory_space=pltpu.VMEM),
            pl.BlockSpec(memory_space=pltpu.VMEM),
        ),
        scratch_shapes=held + scratch,
        compiler_params=pltpu.CompilerParams(
            collective_id=0, has_side_effects=True, vmem_limit_bytes=24 << 20
        ),
        name="decode_step",
    )(*operands)
    return layer_out.astype(BF16), new_state


def solution(mesh):
    placed = (
        P(None, "tp", None),
        P(None, "ctx", "tp", None),
        P(None, "ctx", "tp", None),
        P(),
        P(None, "ctx"),
        P("ctx", "tp"),
        P(),
        P(("ctx", "tp"), None),
        P(("ctx", "tp"), None),
        P(None, ("ctx", "tp")),
        P(("ctx", "tp")),
        P(None, None, ("ctx", "tp")),
        P(("ctx", "tp"), None),
        P(("ctx", "tp"), None),
        P(("ctx", "tp")),
        P(None, ("ctx", "tp")),
        P(("ctx", "tp")),
        P(None, None, ("ctx", "tp")),
        P(("ctx", "tp"), None),
    )
    return jax.shard_map(
        on_device,
        mesh=mesh,
        in_specs=placed,
        out_specs=(P(None, ("ctx", "tp")), P(None, None, ("ctx", "tp"))),
        check_vma=False,
    )
```

```python
import functools

import jax
import jax.numpy as jnp
from jax import lax
from jax.experimental import pallas as pl
from jax.experimental.pallas import tpu as pltpu
from jax.sharding import PartitionSpec as P

MESH = pl.DeviceIdType.MESH
F32 = jnp.float32
BF16 = jnp.bfloat16


def far_first(n):
    return sorted(range(1, n), key=lambda d: -min(d, n - d))


def nt(left, right):
    return lax.dot_general(
        left, right, (((1,), (1,)), ((), ())), preferred_element_type=F32
    )


def silu(x):
    return x * (1.0 / (1.0 + jnp.exp(-x)))


def softplus(x):
    return jnp.maximum(x, 0.0) + jnp.log1p(jnp.exp(-jnp.abs(x)))


def iota(shape, dim):
    return lax.broadcasted_iota(jnp.int32, shape, dim)


def kernel(*refs):
    names_in = (
        "len", "q", "k", "v", "res", "gain", "iw", "gw", "cw", "cb", "cs", "pw",
        "sw", "sb", "dl", "sg", "ss", "outw",
    )
    n_in = len(names_in)
    ow = refs[n_in]
    hbm = dict(zip(names_in, refs[:n_in]))
    lo_ref, ns_ref = refs[n_in + 1 : n_in + 3]
    vm = dict(zip(names_in, refs[n_in + 3 : 2 * n_in + 3]))
    (
        sums, marks, o0, ml0, r_o, r_ml, ob, mlb, attf, wo, hp, r_hp, h2, p_a, r_pa, rank_b, r_rank,
        maps_b, r_maps, tb, td, r_d, in_sem, own_sem, chip_sem, send_sem, recv_sem,
    ) = refs[2 * n_in + 3 :]

    c = lax.axis_index("ctx")
    h = lax.axis_index("tp")
    a = lax.div(c, 16)
    b = lax.rem(c, 16)
    z = lax.div(b, 2)
    core = lax.rem(b, 2)
    e = a * 2 + h

    y, xl = lax.div(a, 2), lax.rem(a, 2)
    rows_of = {
        (dy, dx): lax.rem(y + dy, 4) * 2 + (1 - xl if dx else xl)
        for dy in range(4)
        for dx in range(2)
    }
    rings = [lax.rem(z + dz, 8) for dz in range(8)]
    cores = (core, 1 - core)
    sides = (h, 1 - h)
    offsets = [
        (dy, dx, dz, dc, dh)
        for dy in range(4)
        for dx in range(2)
        for dz in range(8)
        for dc in range(2)
        for dh in range(2)
    ]

    def hops(offset):
        dy, dx, dz, dc, dh = offset
        across = (0, 1, 2, 1)[dh * 2 + dx]
        return min(dy, 4 - dy) + across + min(dz, 8 - dz) + 1.5 * dc

    offsets = sorted(offsets[1:], key=lambda o: -hops(o))

    def peers(which):
        found = []
        for offset in offsets:
            if all(x == 0 or i in which for i, x in enumerate(offset)):
                dy, dx, dz, dc, dh = offset
                row, at = rows_of[dy, dx], rings[dz] * 2 + cores[dc]
                found.append((row, at, sides[dh], (row * 16 + at, sides[dh])))
        return found

    a8, yx, b16 = peers((0, 1)), peers((0, 1, 4)), peers((2, 3))

    loads = {
        name: pltpu.make_async_copy(hbm[name], vm[name], in_sem.at[i])
        for i, name in enumerate(names_in)
    }

    def need(*names):
        for name in names:
            loads.pop(name).wait()

    barrier = pltpu.get_barrier_semaphore()
    greeted = [peer[3] for peer in b16]
    greeted += [peer[3] for peer in a8] + [(c, 1 - h)]
    for peer in greeted:
        pl.semaphore_signal(barrier, 1, device_id=peer, device_id_type=MESH)

    first = ("k", "q", "len", "v")
    for name in first:
        loads[name].start()


    def send(src, dst, stage, peer):
        pltpu.make_async_remote_copy(
            src, dst, send_sem.at[stage], recv_sem.at[stage],
            device_id=peer, device_id_type=MESH,
        ).start()

    def arrived(block, stage):
        pltpu.make_async_copy(block, block, recv_sem.at[stage]).wait()

    pending = []

    def sent(block, stage):
        pltpu.make_async_copy(block, block, send_sem.at[stage]).wait()

    shape = (32, 512)
    column = iota(shape, 1)
    same_head = lax.rem(column, 4) == lax.div(iota(shape, 0), 8)
    position = c * 128 + lax.div(column, 4)
    lane16 = iota((16, 128), 1)
    on_diag = lane16 == iota((16, 128), 0)
    low4 = iota((4, 128), 1) < 64
    need(*first)
    for r in range(4):
        scores = nt(vm["q"][r], vm["k"][r]) * (128.0 ** -0.5)
        live = jnp.logical_and(same_head, position < vm["len"][r])
        scores = jnp.where(live, scores, -1e30)
        high = jnp.max(scores, axis=1, keepdims=True)
        weights = jnp.where(live, jnp.exp(scores - high), 0.0)
        total = jnp.sum(weights, axis=1, keepdims=True)
        summed = jnp.dot(
            weights.astype(BF16), vm["v"][r], preferred_element_type=F32
        )
        for i in range(8):
            rows = slice(i * 4, i * 4 + 4)
            sums[i, r * 4 : r * 4 + 4] = summed[rows]
            marks[i, r * 4 : r * 4 + 4] = jnp.where(low4, high[rows], total[rows])
    at = iota((16, 128), 0)
    on_row = jnp.logical_or(on_diag, lane16 == at + 64)
    for i in range(8):
        o0[i] = sums[i].astype(BF16)
        ml0[i] = jnp.sum(jnp.where(on_row, marks[i], 0.0), axis=0, keepdims=True)

    pl.semaphore_wait(barrier, len(greeted))

    for i, (other, _, _, peer) in enumerate(a8):
        send(ml0.at[other], r_ml.at[i], 0, peer)
        send(o0.at[other], r_o.at[i], 11, peer)
    sent(r_ml.at[pl.ds(0, 7)], 0)
    sent(r_o.at[pl.ds(0, 7)], 11)

    def columns_of(device):
        return ow.at[:, pl.ds(pl.multiple_of(device * 512, 512), 512)]

    mine = wo.at[pl.ds(pl.multiple_of(a * 64, 64), 64)]
    for other, _, _, peer in a8:
        send(columns_of(other), mine, 1, peer)
    pending.append((wo.at[pl.ds(0, 448)], 1))
    own_columns = pltpu.make_async_copy(columns_of(a), mine, own_sem)
    own_columns.start()
    for name in names_in:
        if name not in first:
            loads[name].start()

    def swapped(x):
        return jnp.concatenate([x[:, 64:], x[:, :64]], axis=1)

    low1 = iota((1, 128), 1) < 64
    filled = iota((1, 128), 1) < 16

    def weigh(marks):
        top = jnp.max(marks, axis=0, keepdims=True)
        scales = jnp.exp(marks - top)
        return scales, top, jnp.sum(scales * swapped(marks), axis=0, keepdims=True)

    def column(row):
        return jnp.sum(jnp.where(on_diag, row, 0.0), axis=1, keepdims=True)

    arrived(r_ml.at[pl.ds(0, 7)], 0)
    r_ml[7] = ml0[a]
    scales, top, total = weigh(r_ml[:, 0, :])
    scales = [column(scales[i : i + 1]) for i in range(8)]
    arrived(r_o.at[pl.ds(0, 7)], 11)
    r_o[7] = o0[a]
    summed = sum(scales[i] * r_o[i].astype(F32) for i in range(8))

    ob[b] = summed.astype(BF16)
    mlb[b] = jnp.where(low1, top, swapped(total))
    for _, _, _, peer in b16:
        send(mlb.at[b], mlb.at[b], 2, peer)
        send(ob.at[b], ob.at[b], 3, peer)
    pending.append((mlb.at[pl.ds(0, 15)], 2))
    pending.append((ob.at[pl.ds(0, 15)], 3))
    arrived(mlb.at[pl.ds(0, 15)], 2)
    scales, _, total = weigh(mlb[:, 0, :])
    scales = scales / jnp.where(filled, total, 1.0)
    scales = [column(scales[i : i + 1]) for i in range(16)]
    arrived(ob.at[pl.ds(0, 15)], 3)
    attended = sum(scales[i] * ob[i].astype(F32) for i in range(16))

    for r in range(4):
        attf[r] = attended[r * 4 : r * 4 + 4]
    flat = jnp.concatenate([attf[:, i, :] for i in range(4)], axis=1).astype(BF16)
    need("res")
    own_columns.wait()
    arrived(wo.at[pl.ds(0, 448)], 1)
    partial = nt(flat, wo[...])
    rest = vm["res"][...].astype(F32)
    twice = jnp.concatenate([rest, rest], axis=1)
    adds = jnp.logical_and(low4 == (lax.rem(a, 2) == 0), h == 0)
    rest = jnp.where(adds, twice, 0.0)
    for i in range(4):
        hp[i] = partial[:, i * 128 : i * 128 + 128] + jnp.where(
            lax.div(a, 2) == i, rest, 0.0
        )

    for i, (_, _, _, peer) in enumerate(yx):
        send(hp, r_hp.at[i], 4, peer)
    pending.append((r_hp, 4))
    arrived(r_hp, 4)
    h2[b] = (hp[...] + jnp.sum(r_hp[...], axis=0)).reshape(16, 128).astype(BF16)
    for _, _, _, peer in b16:
        pltpu.make_async_remote_copy(
            h2.at[b], h2.at[b], send_sem.at[5], chip_sem.at[b],
            device_id=peer, device_id_type=MESH,
        ).start()
    pending.append((h2.at[pl.ds(0, 15)], 5))
    need("gain", "iw", "gw", "cw", "cb", "cs", "pw")
    conv = vm["cb"][...]
    for i in range(3):
        conv = conv + vm["cs"][i].astype(F32) * vm["cw"][i : i + 1]

    low16 = lane16 < 64
    squares = jnp.zeros((16, 128), F32)
    inputs = jnp.zeros((4, 64), F32)
    gates = jnp.zeros((4, 64), F32)
    for d in (0, 1, 7, 2, 6, 3, 5, 4):
        chip = lax.rem(z + d, 8)
        awaited = [chip * 2 + core, chip * 2 + 1 - core] if d else [b + 1 - 2 * core]
        for slot in awaited:
            pltpu.make_async_copy(h2.at[slot], h2.at[slot], chip_sem.at[slot]).wait()
        left = h2[2 * chip].astype(F32)
        right = h2[2 * chip + 1].astype(F32)
        even = jnp.where(low16, left, swapped(right))
        odd = jnp.where(low16, swapped(left), right)
        squares = squares + (even * even + odd * odd)
        block = jnp.concatenate(
            [
                (odd if i % 2 else even)[i // 2 * 4 : i // 2 * 4 + 4]
                * vm["gain"][i * 8 + chip]
                for i in range(8)
            ],
            axis=1,
        ).astype(BF16)

        def times(weight):
            part = [
                weight[:, pl.ds(pl.multiple_of(i * 1024 + chip * 128, 128), 128)]
                for i in range(8)
            ]
            return nt(block, jnp.concatenate(part, axis=1))

        inputs = inputs + times(vm["iw"])
        gates = gates + times(vm["gw"])
    squares = jnp.sum(squares, axis=1, keepdims=True)
    square = sum(squares[i * 4 : i * 4 + 4] for i in range(4))
    scale = lax.rsqrt(square * (1.0 / 8192.0) + 1e-5)
    inputs = inputs * scale
    mixed = silu(conv + inputs * vm["cw"][3:4])

    local = jnp.dot(mixed.astype(BF16), vm["pw"][...], preferred_element_type=F32)
    for i in range(4):
        p_a[i] = local[:, i * 128 : i * 128 + 128]
    p_a[4] = jnp.concatenate([local[:, 512:544], jnp.zeros((4, 96), F32)], axis=1)
    for i, (_, _, _, peer) in enumerate(yx):
        send(p_a, r_pa.at[i], 6, peer)
    pending.append((r_pa, 6))
    gates = silu(gates * scale)
    need("sw", "sb", "dl", "sg", "ss", "outw")
    rate = jnp.exp(vm["dl"][...])
    skip = vm["sg"][...] * mixed
    arrived(r_pa, 6)
    projected = p_a[...] + jnp.sum(r_pa[...], axis=0)
    ranks = projected[0:4].reshape(16, 128)
    rank_b[...] = ranks.astype(BF16)
    maps_b[...] = projected[4]
    for i, (_, _, _, peer) in enumerate(b16):
        send(rank_b, r_rank.at[i], 7, peer)
        send(maps_b, r_maps.at[i], 8, peer)
    pending.append((r_rank, 7))
    pending.append((r_maps, 8))
    arrived(r_rank, 7)
    ranks = ranks + jnp.sum(r_rank[...].astype(F32), axis=0)
    arrived(r_maps, 8)
    maps = maps_b[...] + jnp.sum(r_maps[...], axis=0)

    rank = jnp.concatenate(
        [ranks[i * 4 : i * 4 + 4] for i in range(4)], axis=1
    ).astype(BF16)
    step = softplus(nt(rank, vm["sw"][...]) + vm["sb"][...])
    pick_leave = lane16 == iota((16, 128), 0) + 16
    rows = []
    for r in range(4):
        row = maps[r : r + 1]
        entry = jnp.sum(jnp.where(on_diag, row, 0.0), axis=1, keepdims=True)
        leave = jnp.sum(jnp.where(pick_leave, row, 0.0), axis=1, keepdims=True)
        step_r = step[r : r + 1]
        state = jnp.exp(-step_r * rate) * vm["ss"][r] + entry * (step_r * mixed[r : r + 1])
        ns_ref[r] = state
        rows.append(jnp.sum(state * leave, axis=0, keepdims=True))
    gated = ((jnp.concatenate(rows, axis=0) + skip) * gates).astype(BF16)

    term = jnp.dot(gated, vm["outw"][...], preferred_element_type=F32)
    for i in range(64):
        tb[i] = term[:, i * 128 : i * 128 + 128]
    group = lax.div(iota((64, 128), 1), 32)
    spread = [tb[:, r, :] for r in range(4)]
    for q in range(4):
        shares = jnp.zeros((64, 128), F32)
        for r in range(4):
            turn = (q - r) % 4 * 32
            x = spread[r]
            if turn:
                x = jnp.concatenate([x[:, turn:], x[:, :turn]], axis=1)
            shares = jnp.where(group == r, x, shares)
        td[q] = shares.reshape(64, 1, 128)
    for i, (row, at, side, peer) in enumerate(peers((0, 1, 2, 3, 4))):
        share = td.at[lax.rem(at, 2) * 2 + side, row * 8 + lax.div(at, 2)]
        send(share, r_d.at[i], 9, peer)
    pending.append((r_d, 9))
    near = h2[b].astype(F32)
    near = sum(
        jnp.where(lax.div(a, 2) == i, near[i * 4 : i * 4 + 4], 0.0) for i in range(4)
    )
    place = lax.rem(a, 2) * 2 + h
    own = near[:, 0:32]
    for i in range(1, 4):
        own = jnp.where(place == i, near[:, i * 32 : i * 32 + 32], own)
    arrived(r_d, 9)
    whole = td[core * 2 + h, a * 8 + z] + jnp.sum(r_d[...], axis=0)
    shares = [whole[:, r * 32 : r * 32 + 32] for r in range(4)]
    lo_ref[...] = (jnp.concatenate(shares, axis=0) + own).astype(BF16)

    for block, stage in pending:
        sent(block, stage)


def on_device(
    query, keys, values, lengths, residual, out_weight, norm_gain, input_weight,
    gate_weight, conv_weight, conv_bias, conv_state, proj_weight, step_weight,
    step_bias, decay_log, skip_gain, scan_state, output_weight,
):
    operands = (
        lengths,
        query,
        keys.reshape(4, 512, 128),
        values.reshape(4, 512, 128),
        residual,
        norm_gain.reshape(64, 1, 128),
        input_weight,
        gate_weight,
        conv_weight,
        conv_bias.reshape(1, 64),
        conv_state.transpose(1, 0, 2),
        proj_weight,
        step_weight,
        step_bias.reshape(1, 64),
        decay_log,
        skip_gain.reshape(1, 64),
        scan_state,
        output_weight,
    )
    held = [pltpu.SMEM(lengths.shape, lengths.dtype)]
    held += [pltpu.VMEM(x.shape, x.dtype) for x in operands[1:]]
    operands = [
        pltpu.with_memory_space_constraint(x, pltpu.HBM)
        for x in operands + (out_weight,)
    ]
    scratch = [
        pltpu.VMEM((8, 16, 128), F32),
        pltpu.VMEM((8, 16, 128), F32),
        pltpu.VMEM((8, 16, 128), BF16),
        pltpu.VMEM((8, 1, 128), F32),
        pltpu.VMEM((8, 16, 128), BF16),
        pltpu.VMEM((8, 1, 128), F32),
        pltpu.VMEM((16, 16, 128), BF16),
        pltpu.VMEM((16, 1, 128), F32),
        pltpu.VMEM((4, 4, 128), F32),
        pltpu.VMEM((512, 512), BF16),
        pltpu.VMEM((4, 4, 128), F32),
        pltpu.VMEM((15, 4, 4, 128), F32),
        pltpu.VMEM((16, 16, 128), BF16),
        pltpu.VMEM((5, 4, 128), F32),
        pltpu.VMEM((15, 5, 4, 128), F32),
        pltpu.VMEM((16, 128), BF16),
        pltpu.VMEM((15, 16, 128), BF16),
        pltpu.VMEM((4, 128), F32),
        pltpu.VMEM((15, 4, 128), F32),
        pltpu.VMEM((64, 4, 128), F32),
        pltpu.VMEM((4, 64, 1, 128), F32),
        pltpu.VMEM((255, 1, 128), F32),
        pltpu.SemaphoreType.DMA((len(held),)),
        pltpu.SemaphoreType.DMA,
        pltpu.SemaphoreType.DMA((16,)),
        pltpu.SemaphoreType.DMA((12,)),
        pltpu.SemaphoreType.DMA((12,)),
    ]
    layer_out, new_state = pl.pallas_call(
        kernel,
        out_shape=(
            jax.ShapeDtypeStruct((4, 32), BF16),
            jax.ShapeDtypeStruct((4, 16, 64), F32),
        ),
        in_specs=[pl.BlockSpec(memory_space=pltpu.HBM)] * len(operands),
        out_specs=(
            pl.BlockSpec(memory_space=pltpu.VMEM),
            pl.BlockSpec(memory_space=pltpu.VMEM),
        ),
        scratch_shapes=held + scratch,
        compiler_params=pltpu.CompilerParams(
            collective_id=0, has_side_effects=True, vmem_limit_bytes=24 << 20
        ),
        name="decode_step",
    )(*operands)
    return layer_out, new_state


def solution(mesh):
    placed = (
        P(None, "tp", None),
        P(None, "ctx", "tp", None),
        P(None, "ctx", "tp", None),
        P(),
        P(None, "ctx"),
        P("ctx", "tp"),
        P(),
        P(("ctx", "tp"), None),
        P(("ctx", "tp"), None),
        P(None, ("ctx", "tp")),
        P(("ctx", "tp")),
        P(None, None, ("ctx", "tp")),
        P(("ctx", "tp"), None),
        P(("ctx", "tp"), None),
        P(("ctx", "tp")),
        P(None, ("ctx", "tp")),
        P(("ctx", "tp")),
        P(None, None, ("ctx", "tp")),
        P(("ctx", "tp"), None),
    )
    return jax.shard_map(
        on_device,
        mesh=mesh,
        in_specs=placed,
        out_specs=(P(None, ("ctx", "tp")), P(None, None, ("ctx", "tp"))),
        check_vma=False,
    )
```

```python
import functools

import jax
import jax.numpy as jnp
from jax import lax
from jax.experimental import pallas as pl
from jax.experimental.pallas import tpu as pltpu
from jax.sharding import PartitionSpec as P

MESH = pl.DeviceIdType.MESH
F32 = jnp.float32
BF16 = jnp.bfloat16


def far_first(n):
    return sorted(range(1, n), key=lambda d: -min(d, n - d))


def nt(left, right):
    return lax.dot_general(
        left, right, (((1,), (1,)), ((), ())), preferred_element_type=F32
    )


def silu(x):
    return x * (1.0 / (1.0 + jnp.exp(-x)))


def softplus(x):
    return jnp.maximum(x, 0.0) + jnp.log1p(jnp.exp(-jnp.abs(x)))


def iota(shape, dim):
    return lax.broadcasted_iota(jnp.int32, shape, dim)


def kernel(*refs):
    names_in = (
        "len", "q", "k", "v", "res", "gain", "iw", "gw", "cw", "cb", "cs", "pw",
        "sw", "sb", "dl", "sg", "ss", "outw",
    )
    n_in = len(names_in)
    ow = refs[n_in]
    hbm = dict(zip(names_in, refs[:n_in]))
    lo_ref, ns_ref = refs[n_in + 1 : n_in + 3]
    vm = dict(zip(names_in, refs[n_in + 3 : 2 * n_in + 3]))
    (
        sums, marks, o0, ml0, r_o, r_ml, ob, mlb, attf, wo, hp, r_hp, h2, p_a, r_pa, rank_b, r_rank,
        maps_b, r_maps, tb, td, r_d, in_sem, own_sem, chip_sem, send_sem, recv_sem,
    ) = refs[2 * n_in + 3 :]

    c = lax.axis_index("ctx")
    h = lax.axis_index("tp")
    a = lax.div(c, 16)
    b = lax.rem(c, 16)
    z = lax.div(b, 2)
    core = lax.rem(b, 2)
    e = a * 2 + h

    y, xl = lax.div(a, 2), lax.rem(a, 2)
    rows_of = {
        (dy, dx): lax.rem(y + dy, 4) * 2 + (1 - xl if dx else xl)
        for dy in range(4)
        for dx in range(2)
    }
    rings = [lax.rem(z + dz, 8) for dz in range(8)]
    cores = (core, 1 - core)
    sides = (h, 1 - h)
    offsets = [
        (dy, dx, dz, dc, dh)
        for dy in range(4)
        for dx in range(2)
        for dz in range(8)
        for dc in range(2)
        for dh in range(2)
    ]

    def hops(offset):
        dy, dx, dz, dc, dh = offset
        across = (0, 1, 2, 1)[dh * 2 + dx]
        return min(dy, 4 - dy) + across + min(dz, 8 - dz) + 1.5 * dc

    offsets = sorted(offsets[1:], key=lambda o: -hops(o))

    def peers(which):
        found = []
        for offset in offsets:
            if all(x == 0 or i in which for i, x in enumerate(offset)):
                dy, dx, dz, dc, dh = offset
                row, at = rows_of[dy, dx], rings[dz] * 2 + cores[dc]
                found.append((row, at, sides[dh], (row * 16 + at, sides[dh])))
        return found

    a8, yx, b16 = peers((0, 1)), peers((0, 1, 4)), peers((2, 3))

    loads = {
        name: pltpu.make_async_copy(hbm[name], vm[name], in_sem.at[i])
        for i, name in enumerate(names_in)
    }

    def need(*names):
        for name in names:
            loads.pop(name).wait()

    barrier = pltpu.get_barrier_semaphore()
    greeted = [peer[3] for peer in b16]
    greeted += [peer[3] for peer in a8] + [(c, 1 - h)]
    for peer in greeted:
        pl.semaphore_signal(barrier, 1, device_id=peer, device_id_type=MESH)

    first = ("k", "q", "len", "v")
    for name in first:
        loads[name].start()


    def send(src, dst, stage, peer):
        pltpu.make_async_remote_copy(
            src, dst, send_sem.at[stage], recv_sem.at[stage],
            device_id=peer, device_id_type=MESH,
        ).start()

    def arrived(block, stage):
        pltpu.make_async_copy(block, block, recv_sem.at[stage]).wait()

    pending = []

    def sent(block, stage):
        pltpu.make_async_copy(block, block, send_sem.at[stage]).wait()

    shape = (32, 512)
    column = iota(shape, 1)
    same_head = lax.rem(column, 4) == lax.div(iota(shape, 0), 8)
    position = c * 128 + lax.div(column, 4)
    lane16 = iota((16, 128), 1)
    on_diag = lane16 == iota((16, 128), 0)
    low4 = iota((4, 128), 1) < 64
    need(*first)
    for r in range(4):
        scores = nt(vm["q"][r], vm["k"][r]) * (128.0 ** -0.5)
        live = jnp.logical_and(same_head, position < vm["len"][r])
        scores = jnp.where(live, scores, -1e30)
        high = jnp.max(scores, axis=1, keepdims=True)
        weights = jnp.where(live, jnp.exp(scores - high), 0.0)
        total = jnp.sum(weights, axis=1, keepdims=True)
        summed = jnp.dot(
            weights.astype(BF16), vm["v"][r], preferred_element_type=F32
        )
        for i in range(8):
            rows = slice(i * 4, i * 4 + 4)
            sums[i, r * 4 : r * 4 + 4] = summed[rows]
            marks[i, r * 4 : r * 4 + 4] = jnp.where(low4, high[rows], total[rows])
    at = iota((16, 128), 0)
    on_row = jnp.logical_or(on_diag, lane16 == at + 64)
    for i in range(8):
        o0[i] = sums[i].astype(BF16)
        ml0[i] = jnp.sum(jnp.where(on_row, marks[i], 0.0), axis=0, keepdims=True)

    pl.semaphore_wait(barrier, len(greeted))

    for i, (other, _, _, peer) in enumerate(a8):
        send(ml0.at[other], r_ml.at[i], 0, peer)
        send(o0.at[other], r_o.at[i], 11, peer)
    sent(r_ml.at[pl.ds(0, 7)], 0)
    sent(r_o.at[pl.ds(0, 7)], 11)

    def columns_of(device):
        return ow.at[:, pl.ds(pl.multiple_of(device * 512, 512), 512)]

    mine = wo.at[pl.ds(pl.multiple_of(a * 64, 64), 64)]
    for other, _, _, peer in a8[:4]:
        send(columns_of(other), mine, 1, peer)
    own_columns = pltpu.make_async_copy(columns_of(a), mine, own_sem)
    own_columns.start()
    for name in names_in:
        if name not in first:
            loads[name].start()

    def swapped(x):
        return jnp.concatenate([x[:, 64:], x[:, :64]], axis=1)

    low1 = iota((1, 128), 1) < 64
    filled = iota((1, 128), 1) < 16

    def weigh(marks):
        top = jnp.max(marks, axis=0, keepdims=True)
        scales = jnp.exp(marks - top)
        return scales, top, jnp.sum(scales * swapped(marks), axis=0, keepdims=True)

    def column(row):
        return jnp.sum(jnp.where(on_diag, row, 0.0), axis=1, keepdims=True)

    arrived(r_ml.at[pl.ds(0, 7)], 0)
    for other, _, _, peer in a8[4:]:
        send(columns_of(other), mine, 1, peer)
    pending.append((wo.at[pl.ds(0, 448)], 1))
    r_ml[7] = ml0[a]
    scales, top, total = weigh(r_ml[:, 0, :])
    scales = [column(scales[i : i + 1]) for i in range(8)]
    arrived(r_o.at[pl.ds(0, 7)], 11)
    r_o[7] = o0[a]
    summed = sum(scales[i] * r_o[i].astype(F32) for i in range(8))

    ob[b] = summed.astype(BF16)
    mlb[b] = jnp.where(low1, top, swapped(total))
    for _, _, _, peer in b16:
        send(mlb.at[b], mlb.at[b], 2, peer)
        send(ob.at[b], ob.at[b], 3, peer)
    pending.append((mlb.at[pl.ds(0, 15)], 2))
    pending.append((ob.at[pl.ds(0, 15)], 3))
    arrived(mlb.at[pl.ds(0, 15)], 2)
    scales, _, total = weigh(mlb[:, 0, :])
    scales = scales / jnp.where(filled, total, 1.0)
    scales = [column(scales[i : i + 1]) for i in range(16)]
    arrived(ob.at[pl.ds(0, 15)], 3)
    attended = sum(scales[i] * ob[i].astype(F32) for i in range(16))

    for r in range(4):
        attf[r] = attended[r * 4 : r * 4 + 4]
    flat = jnp.concatenate([attf[:, i, :] for i in range(4)], axis=1).astype(BF16)
    need("res")
    own_columns.wait()
    arrived(wo.at[pl.ds(0, 448)], 1)
    partial = nt(flat, wo[...])
    rest = vm["res"][...].astype(F32)
    twice = jnp.concatenate([rest, rest], axis=1)
    adds = jnp.logical_and(low4 == (lax.rem(a, 2) == 0), h == 0)
    rest = jnp.where(adds, twice, 0.0)
    for i in range(4):
        hp[i] = partial[:, i * 128 : i * 128 + 128] + jnp.where(
            lax.div(a, 2) == i, rest, 0.0
        )

    for i, (_, _, _, peer) in enumerate(yx):
        send(hp, r_hp.at[i], 4, peer)
    pending.append((r_hp, 4))
    arrived(r_hp, 4)
    h2[b] = (hp[...] + jnp.sum(r_hp[...], axis=0)).reshape(16, 128).astype(BF16)
    for _, _, _, peer in b16:
        pltpu.make_async_remote_copy(
            h2.at[b], h2.at[b], send_sem.at[5], chip_sem.at[b],
            device_id=peer, device_id_type=MESH,
        ).start()
    pending.append((h2.at[pl.ds(0, 15)], 5))
    need("gain", "iw", "gw", "cw", "cb", "cs", "pw")
    conv = vm["cb"][...]
    for i in range(3):
        conv = conv + vm["cs"][i].astype(F32) * vm["cw"][i : i + 1]

    low16 = lane16 < 64
    squares = jnp.zeros((16, 128), F32)
    inputs = jnp.zeros((4, 64), F32)
    gates = jnp.zeros((4, 64), F32)
    for d in (0, 1, 7, 2, 6, 3, 5, 4):
        chip = lax.rem(z + d, 8)
        awaited = [chip * 2 + core, chip * 2 + 1 - core] if d else [b + 1 - 2 * core]
        for slot in awaited:
            pltpu.make_async_copy(h2.at[slot], h2.at[slot], chip_sem.at[slot]).wait()
        left = h2[2 * chip].astype(F32)
        right = h2[2 * chip + 1].astype(F32)
        even = jnp.where(low16, left, swapped(right))
        odd = jnp.where(low16, swapped(left), right)
        squares = squares + (even * even + odd * odd)
        block = jnp.concatenate(
            [
                (odd if i % 2 else even)[i // 2 * 4 : i // 2 * 4 + 4]
                * vm["gain"][i * 8 + chip]
                for i in range(8)
            ],
            axis=1,
        ).astype(BF16)

        def times(weight):
            part = [
                weight[:, pl.ds(pl.multiple_of(i * 1024 + chip * 128, 128), 128)]
                for i in range(8)
            ]
            return nt(block, jnp.concatenate(part, axis=1))

        inputs = inputs + times(vm["iw"])
        gates = gates + times(vm["gw"])
    squares = jnp.sum(squares, axis=1, keepdims=True)
    square = sum(squares[i * 4 : i * 4 + 4] for i in range(4))
    scale = lax.rsqrt(square * (1.0 / 8192.0) + 1e-5)
    inputs = inputs * scale
    mixed = silu(conv + inputs * vm["cw"][3:4])

    local = jnp.dot(mixed.astype(BF16), vm["pw"][...], preferred_element_type=F32)
    for i in range(4):
        p_a[i] = local[:, i * 128 : i * 128 + 128]
    p_a[4] = jnp.concatenate([local[:, 512:544], jnp.zeros((4, 96), F32)], axis=1)
    for i, (_, _, _, peer) in enumerate(yx):
        send(p_a, r_pa.at[i], 6, peer)
    pending.append((r_pa, 6))
    gates = silu(gates * scale)
    need("sw", "sb", "dl", "sg", "ss", "outw")
    rate = jnp.exp(vm["dl"][...])
    skip = vm["sg"][...] * mixed
    arrived(r_pa, 6)
    projected = p_a[...] + jnp.sum(r_pa[...], axis=0)
    ranks = projected[0:4].reshape(16, 128)
    rank_b[...] = ranks.astype(BF16)
    maps_b[...] = projected[4]
    for i, (_, _, _, peer) in enumerate(b16):
        send(rank_b, r_rank.at[i], 7, peer)
        send(maps_b, r_maps.at[i], 8, peer)
    pending.append((r_rank, 7))
    pending.append((r_maps, 8))
    arrived(r_rank, 7)
    ranks = ranks + jnp.sum(r_rank[...].astype(F32), axis=0)
    arrived(r_maps, 8)
    maps = maps_b[...] + jnp.sum(r_maps[...], axis=0)

    rank = jnp.concatenate(
        [ranks[i * 4 : i * 4 + 4] for i in range(4)], axis=1
    ).astype(BF16)
    step = softplus(nt(rank, vm["sw"][...]) + vm["sb"][...])
    pick_leave = lane16 == iota((16, 128), 0) + 16
    rows = []
    for r in range(4):
        row = maps[r : r + 1]
        entry = jnp.sum(jnp.where(on_diag, row, 0.0), axis=1, keepdims=True)
        leave = jnp.sum(jnp.where(pick_leave, row, 0.0), axis=1, keepdims=True)
        step_r = step[r : r + 1]
        state = jnp.exp(-step_r * rate) * vm["ss"][r] + entry * (step_r * mixed[r : r + 1])
        ns_ref[r] = state
        rows.append(jnp.sum(state * leave, axis=0, keepdims=True))
    gated = ((jnp.concatenate(rows, axis=0) + skip) * gates).astype(BF16)

    term = jnp.dot(gated, vm["outw"][...], preferred_element_type=F32)
    for i in range(64):
        tb[i] = term[:, i * 128 : i * 128 + 128]
    group = lax.div(iota((64, 128), 1), 32)
    spread = [tb[:, r, :] for r in range(4)]
    for q in range(4):
        shares = jnp.zeros((64, 128), F32)
        for r in range(4):
            turn = (q - r) % 4 * 32
            x = spread[r]
            if turn:
                x = jnp.concatenate([x[:, turn:], x[:, :turn]], axis=1)
            shares = jnp.where(group == r, x, shares)
        td[q] = shares.reshape(64, 1, 128)
    for i, (row, at, side, peer) in enumerate(peers((0, 1, 2, 3, 4))):
        share = td.at[lax.rem(at, 2) * 2 + side, row * 8 + lax.div(at, 2)]
        send(share, r_d.at[i], 9, peer)
    pending.append((r_d, 9))
    near = h2[b].astype(F32)
    near = sum(
        jnp.where(lax.div(a, 2) == i, near[i * 4 : i * 4 + 4], 0.0) for i in range(4)
    )
    place = lax.rem(a, 2) * 2 + h
    own = near[:, 0:32]
    for i in range(1, 4):
        own = jnp.where(place == i, near[:, i * 32 : i * 32 + 32], own)
    arrived(r_d, 9)
    whole = td[core * 2 + h, a * 8 + z] + jnp.sum(r_d[...], axis=0)
    shares = [whole[:, r * 32 : r * 32 + 32] for r in range(4)]
    lo_ref[...] = (jnp.concatenate(shares, axis=0) + own).astype(BF16)

    for block, stage in pending:
        sent(block, stage)


def on_device(
    query, keys, values, lengths, residual, out_weight, norm_gain, input_weight,
    gate_weight, conv_weight, conv_bias, conv_state, proj_weight, step_weight,
    step_bias, decay_log, skip_gain, scan_state, output_weight,
):
    operands = (
        lengths,
        query,
        keys.reshape(4, 512, 128),
        values.reshape(4, 512, 128),
        residual,
        norm_gain.reshape(64, 1, 128),
        input_weight,
        gate_weight,
        conv_weight,
        conv_bias.reshape(1, 64),
        conv_state.transpose(1, 0, 2),
        proj_weight,
        step_weight,
        step_bias.reshape(1, 64),
        decay_log,
        skip_gain.reshape(1, 64),
        scan_state,
        output_weight,
    )
    held = [pltpu.SMEM(lengths.shape, lengths.dtype)]
    held += [pltpu.VMEM(x.shape, x.dtype) for x in operands[1:]]
    operands = [
        pltpu.with_memory_space_constraint(x, pltpu.HBM)
        for x in operands + (out_weight,)
    ]
    scratch = [
        pltpu.VMEM((8, 16, 128), F32),
        pltpu.VMEM((8, 16, 128), F32),
        pltpu.VMEM((8, 16, 128), BF16),
        pltpu.VMEM((8, 1, 128), F32),
        pltpu.VMEM((8, 16, 128), BF16),
        pltpu.VMEM((8, 1, 128), F32),
        pltpu.VMEM((16, 16, 128), BF16),
        pltpu.VMEM((16, 1, 128), F32),
        pltpu.VMEM((4, 4, 128), F32),
        pltpu.VMEM((512, 512), BF16),
        pltpu.VMEM((4, 4, 128), F32),
        pltpu.VMEM((15, 4, 4, 128), F32),
        pltpu.VMEM((16, 16, 128), BF16),
        pltpu.VMEM((5, 4, 128), F32),
        pltpu.VMEM((15, 5, 4, 128), F32),
        pltpu.VMEM((16, 128), BF16),
        pltpu.VMEM((15, 16, 128), BF16),
        pltpu.VMEM((4, 128), F32),
        pltpu.VMEM((15, 4, 128), F32),
        pltpu.VMEM((64, 4, 128), F32),
        pltpu.VMEM((4, 64, 1, 128), F32),
        pltpu.VMEM((255, 1, 128), F32),
        pltpu.SemaphoreType.DMA((len(held),)),
        pltpu.SemaphoreType.DMA,
        pltpu.SemaphoreType.DMA((16,)),
        pltpu.SemaphoreType.DMA((12,)),
        pltpu.SemaphoreType.DMA((12,)),
    ]
    layer_out, new_state = pl.pallas_call(
        kernel,
        out_shape=(
            jax.ShapeDtypeStruct((4, 32), BF16),
            jax.ShapeDtypeStruct((4, 16, 64), F32),
        ),
        in_specs=[pl.BlockSpec(memory_space=pltpu.HBM)] * len(operands),
        out_specs=(
            pl.BlockSpec(memory_space=pltpu.VMEM),
            pl.BlockSpec(memory_space=pltpu.VMEM),
        ),
        scratch_shapes=held + scratch,
        compiler_params=pltpu.CompilerParams(
            collective_id=0, has_side_effects=True, vmem_limit_bytes=24 << 20
        ),
        name="decode_step",
    )(*operands)
    return layer_out, new_state


def solution(mesh):
    placed = (
        P(None, "tp", None),
        P(None, "ctx", "tp", None),
        P(None, "ctx", "tp", None),
        P(),
        P(None, "ctx"),
        P("ctx", "tp"),
        P(),
        P(("ctx", "tp"), None),
        P(("ctx", "tp"), None),
        P(None, ("ctx", "tp")),
        P(("ctx", "tp")),
        P(None, None, ("ctx", "tp")),
        P(("ctx", "tp"), None),
        P(("ctx", "tp"), None),
        P(("ctx", "tp")),
        P(None, ("ctx", "tp")),
        P(("ctx", "tp")),
        P(None, None, ("ctx", "tp")),
        P(("ctx", "tp"), None),
    )
    return jax.shard_map(
        on_device,
        mesh=mesh,
        in_specs=placed,
        out_specs=(P(None, ("ctx", "tp")), P(None, None, ("ctx", "tp"))),
        check_vma=False,
    )
```

```python
import functools

import jax
import jax.numpy as jnp
from jax import lax
from jax.experimental import pallas as pl
from jax.experimental.pallas import tpu as pltpu
from jax.sharding import PartitionSpec as P

MESH = pl.DeviceIdType.MESH
F32 = jnp.float32
BF16 = jnp.bfloat16


def far_first(n):
    return sorted(range(1, n), key=lambda d: -min(d, n - d))


def nt(left, right):
    return lax.dot_general(
        left, right, (((1,), (1,)), ((), ())), preferred_element_type=F32
    )


def silu(x):
    return x * (1.0 / (1.0 + jnp.exp(-x)))


def softplus(x):
    return jnp.maximum(x, 0.0) + jnp.log1p(jnp.exp(-jnp.abs(x)))


def iota(shape, dim):
    return lax.broadcasted_iota(jnp.int32, shape, dim)


def kernel(*refs):
    names_in = (
        "len", "q", "k", "v", "res", "gain", "iw", "gw", "cw", "cb", "cs", "pw",
        "sw", "sb", "dl", "sg", "ss", "outw",
    )
    n_in = len(names_in)
    ow = refs[n_in]
    hbm = dict(zip(names_in, refs[:n_in]))
    lo_ref, ns_ref = refs[n_in + 1 : n_in + 3]
    vm = dict(zip(names_in, refs[n_in + 3 : 2 * n_in + 3]))
    (
        sums, marks, o0, ml0, r_o, r_ml, ob, mlb, attf, wo, hp, r_hp, h2, p_a, r_pa, rank_b, r_rank,
        maps_b, r_maps, tb, td, r_d, in_sem, own_sem, chip_sem, send_sem, recv_sem,
    ) = refs[2 * n_in + 3 :]

    c = lax.axis_index("ctx")
    h = lax.axis_index("tp")
    a = lax.div(c, 16)
    b = lax.rem(c, 16)
    z = lax.div(b, 2)
    core = lax.rem(b, 2)
    e = a * 2 + h

    y, xl = lax.div(a, 2), lax.rem(a, 2)
    rows_of = {
        (dy, dx): lax.rem(y + dy, 4) * 2 + (1 - xl if dx else xl)
        for dy in range(4)
        for dx in range(2)
    }
    rings = [lax.rem(z + dz, 8) for dz in range(8)]
    cores = (core, 1 - core)
    sides = (h, 1 - h)
    offsets = [
        (dy, dx, dz, dc, dh)
        for dy in range(4)
        for dx in range(2)
        for dz in range(8)
        for dc in range(2)
        for dh in range(2)
    ]

    def hops(offset):
        dy, dx, dz, dc, dh = offset
        across = (0, 1, 2, 1)[dh * 2 + dx]
        return min(dy, 4 - dy) + across + min(dz, 8 - dz) + 1.5 * dc

    offsets = sorted(offsets[1:], key=lambda o: -hops(o))

    def peers(which):
        found = []
        for offset in offsets:
            if all(x == 0 or i in which for i, x in enumerate(offset)):
                dy, dx, dz, dc, dh = offset
                row, at = rows_of[dy, dx], rings[dz] * 2 + cores[dc]
                found.append((row, at, sides[dh], (row * 16 + at, sides[dh])))
        return found

    a8, yx, b16 = peers((0, 1)), peers((0, 1, 4)), peers((2, 3))

    loads = {
        name: pltpu.make_async_copy(hbm[name], vm[name], in_sem.at[i])
        for i, name in enumerate(names_in)
    }

    def need(*names):
        for name in names:
            loads.pop(name).wait()

    barrier = pltpu.get_barrier_semaphore()
    greeted = [peer[3] for peer in b16]
    greeted += [peer[3] for peer in a8] + [(c, 1 - h)]
    for peer in greeted:
        pl.semaphore_signal(barrier, 1, device_id=peer, device_id_type=MESH)

    first = ("k", "q", "len", "v")
    for name in first:
        loads[name].start()


    def send(src, dst, stage, peer):
        pltpu.make_async_remote_copy(
            src, dst, send_sem.at[stage], recv_sem.at[stage],
            device_id=peer, device_id_type=MESH,
        ).start()

    def arrived(block, stage):
        pltpu.make_async_copy(block, block, recv_sem.at[stage]).wait()

    pending = []

    def sent(block, stage):
        pltpu.make_async_copy(block, block, send_sem.at[stage]).wait()

    shape = (32, 512)
    column = iota(shape, 1)
    same_head = lax.rem(column, 4) == lax.div(iota(shape, 0), 8)
    position = c * 128 + lax.div(column, 4)
    lane16 = iota((16, 128), 1)
    on_diag = lane16 == iota((16, 128), 0)
    low4 = iota((4, 128), 1) < 64
    need(*first)
    for r in range(4):
        scores = nt(vm["q"][r], vm["k"][r]) * (128.0 ** -0.5)
        live = jnp.logical_and(same_head, position < vm["len"][r])
        scores = jnp.where(live, scores, -1e30)
        high = jnp.max(scores, axis=1, keepdims=True)
        weights = jnp.where(live, jnp.exp(scores - high), 0.0)
        total = jnp.sum(weights, axis=1, keepdims=True)
        summed = jnp.dot(
            weights.astype(BF16), vm["v"][r], preferred_element_type=F32
        )
        for i in range(8):
            rows = slice(i * 4, i * 4 + 4)
            sums[i, r * 4 : r * 4 + 4] = summed[rows]
            marks[i, r * 4 : r * 4 + 4] = jnp.where(low4, high[rows], total[rows])
    at = iota((16, 128), 0)
    on_row = jnp.logical_or(on_diag, lane16 == at + 64)
    for i in range(8):
        o0[i] = sums[i].astype(BF16)
        ml0[i] = jnp.sum(jnp.where(on_row, marks[i], 0.0), axis=0, keepdims=True)

    pl.semaphore_wait(barrier, len(greeted))

    for i, (other, _, _, peer) in enumerate(a8):
        send(ml0.at[other], r_ml.at[i], 0, peer)
        send(o0.at[other], r_o.at[i], 11, peer)
    sent(r_ml.at[pl.ds(0, 7)], 0)
    sent(r_o.at[pl.ds(0, 7)], 11)

    def columns_of(device):
        return ow.at[:, pl.ds(pl.multiple_of(device * 512, 512), 512)]

    mine = wo.at[pl.ds(pl.multiple_of(a * 64, 64), 64)]
    for other, _, _, peer in a8[:4]:
        send(columns_of(other), mine, 1, peer)
    own_columns = pltpu.make_async_copy(columns_of(a), mine, own_sem)
    own_columns.start()
    for name in names_in:
        if name not in first:
            loads[name].start()

    def swapped(x):
        return jnp.concatenate([x[:, 64:], x[:, :64]], axis=1)

    low1 = iota((1, 128), 1) < 64
    filled = iota((1, 128), 1) < 16

    def weigh(marks):
        top = jnp.max(marks, axis=0, keepdims=True)
        scales = jnp.exp(marks - top)
        return scales, top, jnp.sum(scales * swapped(marks), axis=0, keepdims=True)

    def column(row):
        return jnp.sum(jnp.where(on_diag, row, 0.0), axis=1, keepdims=True)

    arrived(r_ml.at[pl.ds(0, 7)], 0)
    for other, _, _, peer in a8[4:]:
        send(columns_of(other), mine, 1, peer)
    pending.append((wo.at[pl.ds(0, 448)], 1))
    r_ml[7] = ml0[a]
    scales, top, total = weigh(r_ml[:, 0, :])
    scales = [column(scales[i : i + 1]) for i in range(8)]
    arrived(r_o.at[pl.ds(0, 7)], 11)
    r_o[7] = o0[a]
    summed = sum(scales[i] * r_o[i].astype(F32) for i in range(8))

    ob[b] = summed.astype(BF16)
    mlb[b] = jnp.where(low1, top, swapped(total))
    for _, _, _, peer in b16:
        send(mlb.at[b], mlb.at[b], 2, peer)
        send(ob.at[b], ob.at[b], 3, peer)
    pending.append((mlb.at[pl.ds(0, 15)], 2))
    pending.append((ob.at[pl.ds(0, 15)], 3))
    arrived(mlb.at[pl.ds(0, 15)], 2)
    scales, _, total = weigh(mlb[:, 0, :])
    scales = scales / jnp.where(filled, total, 1.0)
    scales = [column(scales[i : i + 1]) for i in range(16)]
    arrived(ob.at[pl.ds(0, 15)], 3)
    attended = sum(scales[i] * ob[i].astype(F32) for i in range(16))

    for r in range(4):
        attf[r] = attended[r * 4 : r * 4 + 4]
    flat = jnp.concatenate([attf[:, i, :] for i in range(4)], axis=1).astype(BF16)
    need("res")
    own_columns.wait()
    arrived(wo.at[pl.ds(0, 448)], 1)
    partial = nt(flat, wo[...])
    rest = vm["res"][...].astype(F32)
    twice = jnp.concatenate([rest, rest], axis=1)
    adds = jnp.logical_and(low4 == (lax.rem(a, 2) == 0), h == 0)
    rest = jnp.where(adds, twice, 0.0)
    partial = jnp.concatenate(
        [
            partial[:, i * 128 : i * 128 + 128]
            + jnp.where(lax.div(a, 2) == i, rest, 0.0)
            for i in range(4)
        ],
        axis=0,
    )
    hp[...] = partial.astype(BF16)

    for i, (_, _, _, peer) in enumerate(yx):
        send(hp, r_hp.at[i], 4, peer)
    pending.append((r_hp, 4))
    arrived(r_hp, 4)
    h2[b] = (partial + jnp.sum(r_hp[...].astype(F32), axis=0)).astype(BF16)
    for _, _, _, peer in b16:
        pltpu.make_async_remote_copy(
            h2.at[b], h2.at[b], send_sem.at[5], chip_sem.at[b],
            device_id=peer, device_id_type=MESH,
        ).start()
    pending.append((h2.at[pl.ds(0, 15)], 5))
    need("gain", "iw", "gw", "cw", "cb", "cs", "pw")
    conv = vm["cb"][...]
    for i in range(3):
        conv = conv + vm["cs"][i].astype(F32) * vm["cw"][i : i + 1]

    low16 = lane16 < 64
    squares = jnp.zeros((16, 128), F32)
    inputs = jnp.zeros((4, 64), F32)
    gates = jnp.zeros((4, 64), F32)
    for d in (0, 1, 7, 2, 6, 3, 5, 4):
        chip = lax.rem(z + d, 8)
        awaited = [chip * 2 + core, chip * 2 + 1 - core] if d else [b + 1 - 2 * core]
        for slot in awaited:
            pltpu.make_async_copy(h2.at[slot], h2.at[slot], chip_sem.at[slot]).wait()
        left = h2[2 * chip].astype(F32)
        right = h2[2 * chip + 1].astype(F32)
        even = jnp.where(low16, left, swapped(right))
        odd = jnp.where(low16, swapped(left), right)
        squares = squares + (even * even + odd * odd)
        block = jnp.concatenate(
            [
                (odd if i % 2 else even)[i // 2 * 4 : i // 2 * 4 + 4]
                * vm["gain"][i * 8 + chip]
                for i in range(8)
            ],
            axis=1,
        ).astype(BF16)

        def times(weight):
            part = [
                weight[:, pl.ds(pl.multiple_of(i * 1024 + chip * 128, 128), 128)]
                for i in range(8)
            ]
            return nt(block, jnp.concatenate(part, axis=1))

        inputs = inputs + times(vm["iw"])
        gates = gates + times(vm["gw"])
    squares = jnp.sum(squares, axis=1, keepdims=True)
    square = sum(squares[i * 4 : i * 4 + 4] for i in range(4))
    scale = lax.rsqrt(square * (1.0 / 8192.0) + 1e-5)
    inputs = inputs * scale
    mixed = silu(conv + inputs * vm["cw"][3:4])

    local = jnp.dot(mixed.astype(BF16), vm["pw"][...], preferred_element_type=F32)
    for i in range(4):
        p_a[i] = local[:, i * 128 : i * 128 + 128]
    p_a[4] = jnp.concatenate([local[:, 512:544], jnp.zeros((4, 96), F32)], axis=1)
    for i, (_, _, _, peer) in enumerate(yx):
        send(p_a, r_pa.at[i], 6, peer)
    pending.append((r_pa, 6))
    gates = silu(gates * scale)
    need("sw", "sb", "dl", "sg", "ss", "outw")
    rate = jnp.exp(vm["dl"][...])
    skip = vm["sg"][...] * mixed
    arrived(r_pa, 6)
    projected = p_a[...] + jnp.sum(r_pa[...], axis=0)
    ranks = projected[0:4].reshape(16, 128)
    rank_b[...] = ranks.astype(BF16)
    maps_b[...] = jnp.concatenate(
        [projected[4, r : r + 1, 0:32] for r in range(4)], axis=1
    )
    for i, (_, _, _, peer) in enumerate(b16):
        send(rank_b, r_rank.at[i], 7, peer)
        send(maps_b, r_maps.at[i], 8, peer)
    pending.append((r_rank, 7))
    pending.append((r_maps, 8))
    arrived(r_rank, 7)
    ranks = ranks + jnp.sum(r_rank[...].astype(F32), axis=0)
    arrived(r_maps, 8)
    maps = maps_b[...] + jnp.sum(r_maps[...], axis=0)

    rank = jnp.concatenate(
        [ranks[i * 4 : i * 4 + 4] for i in range(4)], axis=1
    ).astype(BF16)
    step = softplus(nt(rank, vm["sw"][...]) + vm["sb"][...])
    state_row = iota((16, 128), 0)
    rows = []
    for r in range(4):
        pick = lane16 == state_row + r * 32
        entry = jnp.sum(jnp.where(pick, maps, 0.0), axis=1, keepdims=True)
        pick = lane16 == state_row + r * 32 + 16
        leave = jnp.sum(jnp.where(pick, maps, 0.0), axis=1, keepdims=True)
        step_r = step[r : r + 1]
        state = jnp.exp(-step_r * rate) * vm["ss"][r] + entry * (step_r * mixed[r : r + 1])
        ns_ref[r] = state
        rows.append(jnp.sum(state * leave, axis=0, keepdims=True))
    gated = ((jnp.concatenate(rows, axis=0) + skip) * gates).astype(BF16)

    term = jnp.dot(gated, vm["outw"][...], preferred_element_type=F32)
    for i in range(64):
        tb[i] = term[:, i * 128 : i * 128 + 128]
    group = lax.div(iota((64, 128), 1), 32)
    spread = [tb[:, r, :] for r in range(4)]
    for q in range(4):
        shares = jnp.zeros((64, 128), F32)
        for r in range(4):
            turn = (q - r) % 4 * 32
            x = spread[r]
            if turn:
                x = jnp.concatenate([x[:, turn:], x[:, :turn]], axis=1)
            shares = jnp.where(group == r, x, shares)
        td[q] = shares.reshape(64, 1, 128)
    for i, (row, at, side, peer) in enumerate(peers((0, 1, 2, 3, 4))):
        share = td.at[lax.rem(at, 2) * 2 + side, row * 8 + lax.div(at, 2)]
        send(share, r_d.at[i], 9, peer)
    pending.append((r_d, 9))
    near = h2[b].astype(F32)
    near = sum(
        jnp.where(lax.div(a, 2) == i, near[i * 4 : i * 4 + 4], 0.0) for i in range(4)
    )
    place = lax.rem(a, 2) * 2 + h
    own = near[:, 0:32]
    for i in range(1, 4):
        own = jnp.where(place == i, near[:, i * 32 : i * 32 + 32], own)
    arrived(r_d, 9)
    whole = td[core * 2 + h, a * 8 + z] + jnp.sum(r_d[...], axis=0)
    shares = [whole[:, r * 32 : r * 32 + 32] for r in range(4)]
    lo_ref[...] = (jnp.concatenate(shares, axis=0) + own).astype(BF16)

    for block, stage in pending:
        sent(block, stage)


def on_device(
    query, keys, values, lengths, residual, out_weight, norm_gain, input_weight,
    gate_weight, conv_weight, conv_bias, conv_state, proj_weight, step_weight,
    step_bias, decay_log, skip_gain, scan_state, output_weight,
):
    operands = (
        lengths,
        query,
        keys.reshape(4, 512, 128),
        values.reshape(4, 512, 128),
        residual,
        norm_gain.reshape(64, 1, 128),
        input_weight,
        gate_weight,
        conv_weight,
        conv_bias.reshape(1, 64),
        conv_state.transpose(1, 0, 2),
        proj_weight,
        step_weight,
        step_bias.reshape(1, 64),
        decay_log,
        skip_gain.reshape(1, 64),
        scan_state,
        output_weight,
    )
    held = [pltpu.SMEM(lengths.shape, lengths.dtype)]
    held += [pltpu.VMEM(x.shape, x.dtype) for x in operands[1:]]
    operands = [
        pltpu.with_memory_space_constraint(x, pltpu.HBM)
        for x in operands + (out_weight,)
    ]
    scratch = [
        pltpu.VMEM((8, 16, 128), F32),
        pltpu.VMEM((8, 16, 128), F32),
        pltpu.VMEM((8, 16, 128), BF16),
        pltpu.VMEM((8, 1, 128), F32),
        pltpu.VMEM((8, 16, 128), BF16),
        pltpu.VMEM((8, 1, 128), F32),
        pltpu.VMEM((16, 16, 128), BF16),
        pltpu.VMEM((16, 1, 128), F32),
        pltpu.VMEM((4, 4, 128), F32),
        pltpu.VMEM((512, 512), BF16),
        pltpu.VMEM((16, 128), BF16),
        pltpu.VMEM((15, 16, 128), BF16),
        pltpu.VMEM((16, 16, 128), BF16),
        pltpu.VMEM((5, 4, 128), F32),
        pltpu.VMEM((15, 5, 4, 128), F32),
        pltpu.VMEM((16, 128), BF16),
        pltpu.VMEM((15, 16, 128), BF16),
        pltpu.VMEM((1, 128), F32),
        pltpu.VMEM((15, 1, 128), F32),
        pltpu.VMEM((64, 4, 128), F32),
        pltpu.VMEM((4, 64, 1, 128), F32),
        pltpu.VMEM((255, 1, 128), F32),
        pltpu.SemaphoreType.DMA((len(held),)),
        pltpu.SemaphoreType.DMA,
        pltpu.SemaphoreType.DMA((16,)),
        pltpu.SemaphoreType.DMA((12,)),
        pltpu.SemaphoreType.DMA((12,)),
    ]
    layer_out, new_state = pl.pallas_call(
        kernel,
        out_shape=(
            jax.ShapeDtypeStruct((4, 32), BF16),
            jax.ShapeDtypeStruct((4, 16, 64), F32),
        ),
        in_specs=[pl.BlockSpec(memory_space=pltpu.HBM)] * len(operands),
        out_specs=(
            pl.BlockSpec(memory_space=pltpu.VMEM),
            pl.BlockSpec(memory_space=pltpu.VMEM),
        ),
        scratch_shapes=held + scratch,
        compiler_params=pltpu.CompilerParams(
            collective_id=0, has_side_effects=True, vmem_limit_bytes=24 << 20
        ),
        name="decode_step",
    )(*operands)
    return layer_out, new_state


def solution(mesh):
    placed = (
        P(None, "tp", None),
        P(None, "ctx", "tp", None),
        P(None, "ctx", "tp", None),
        P(),
        P(None, "ctx"),
        P("ctx", "tp"),
        P(),
        P(("ctx", "tp"), None),
        P(("ctx", "tp"), None),
        P(None, ("ctx", "tp")),
        P(("ctx", "tp")),
        P(None, None, ("ctx", "tp")),
        P(("ctx", "tp"), None),
        P(("ctx", "tp"), None),
        P(("ctx", "tp")),
        P(None, ("ctx", "tp")),
        P(("ctx", "tp")),
        P(None, None, ("ctx", "tp")),
        P(("ctx", "tp"), None),
    )
    return jax.shard_map(
        on_device,
        mesh=mesh,
        in_specs=placed,
        out_specs=(P(None, ("ctx", "tp")), P(None, None, ("ctx", "tp"))),
        check_vma=False,
    )
```
